512 devices in a mesh: gx: 32 (over x, z), gy: 16 (over y, core).
Axes of the slice: x: 4, y: 8, z: 8, core: 2. Of those that a mesh axis runs over, the one named last changes fastest.
Arguments:
- voxels: bfloat16 [256, 128, 8, 96], P('gx', 'gy'), may hold values from -6 to 6
- occupancy: int32 [256, 128, 8], P('gx', 'gy'), may hold values 0 or 1
- conv_weight: bfloat16 [27, 96, 96], replicated, may hold values from -0.125 to 0.125
- conv_bias: float32 [96], replicated, may hold values from -3 to 3
- down_weight: bfloat16 [27, 96, 96], replicated, may hold values from -0.125 to 0.125
- down_cotangent: bfloat16 [128, 64, 4, 96], P('gx', 'gy'), may hold values from -6 to 6
Outputs:
- down: bfloat16 [128, 64, 4, 96], P('gx', 'gy')
- grad_voxels: bfloat16 [256, 128, 8, 96], P('gx', 'gy')
- grad_conv: float32 [27, 96, 96], replicated
- grad_bias: float32 [96], replicated
- grad_down: float32 [27, 96, 96], replicated
The draws below stay inside these ranges and needn't reach their ends.
Inputs may be any that keep to these rules, and one draw needn't show every extreme that they name: `occupancy`: 0 or 1 for every voxel.
All inputs are finite; a program needn't handle non-finite values. No bound on the sum of `occupancy` on one device may be relied on, other than what follows from the above.
Results may differ from the reference program's by a relative error of at most 0.006.
Values may be sent and summed in bfloat16 or wider, within the bound.
A program may use at most 64 MiB of HBM per device.

```python
import math
import jax
import jax.numpy as jnp
from jax import lax

C = 96
TAPS = 27
H = 8
NX = 256
NY = 128


def place_ends(entries, stream_key, least, high):
    spot = [jax.random.randint(jax.random.fold_in(stream_key, axis), (), 0, length) for axis, length in enumerate(entries.shape)]
    main_axis = entries.shape.index(max(entries.shape))
    neighbour = spot[:main_axis] + [(spot[main_axis] + 1) % entries.shape[main_axis]] + spot[main_axis + 1:]
    return entries.at[tuple(spot)].set(least).at[tuple(neighbour)].set(high)


def levels(rng, shape, split, low, top_value):
    def one(position, parts):
        draws = jax.random.uniform(jax.random.fold_in(jax.random.fold_in(rng, 6), position), (parts,), jnp.float32, low / len(split), top_value / len(split))
        return jnp.repeat(jnp.exp(draws), shape[position] // parts).reshape((-1,) + (1,) * (len(shape) - position - 1))

    factor_of = one(*split[0])
    for cut in split[1:]:
        factor_of = factor_of * one(*cut)
    return factor_of


def centred(own_key, dims, scale, limit, cuts=(), kind=jnp.bfloat16):
    array = scale * jax.random.normal(own_key, dims, jnp.float32)
    if cuts:
        array = array * levels(own_key, dims, cuts, -0.22, 0.18)
    return jnp.clip(array, -limit, limit).astype(kind)


def setup_inputs(seed: int = 0) -> dict:
    splits = jax.random.split(jax.random.key(seed), 7)
    return {
        "voxels": centred(splits[0], (NX, NY, H, C), 1.0, 6.0, ((0, 32), (1, 16))),
        "occupancy": place_ends((jax.random.randint(splits[1], (NX, NY, H), 0, 2) < 1).astype(jnp.int32), jax.random.fold_in(splits[1], 1), 0, 1),
        "conv_weight": centred(splits[2], (TAPS, C, C), (TAPS * C) ** -0.5, 0.125),
        "conv_bias": centred(splits[3], (C,), 0.5, 3.0, (), jnp.float32),
        "down_weight": centred(splits[4], (TAPS, C, C), (TAPS * C) ** -0.5, 0.125),
        "down_cotangent": centred(splits[5], (NX // 2, NY // 2, H // 2, C), 1.0, 6.0, ((0, 32), (1, 16))),
    }


TAP_OFFSETS = [(step_x, step_y, step_z) for step_x in (-1, 0, 1) for step_y in (-1, 0, 1) for step_z in (-1, 0, 1)]
PARITY_TERMS = {0: [(0, 0)], 1: [(1, 0), (-1, 1)]}

def conv_same(padded, weight, size_x, size_y, size_z):
    channels = padded.shape[-1]
    running = jnp.zeros((size_x * size_y * size_z, weight.shape[2]), jnp.float32)
    for tap_index, (step_x, step_y, step_z) in enumerate(TAP_OFFSETS):
        window = padded[1 + step_x:1 + step_x + size_x, 1 + step_y:1 + step_y + size_y, 1 + step_z:1 + step_z + size_z]
        running = running + jnp.dot(window.reshape(-1, channels), weight[tap_index], preferred_element_type=jnp.float32)
    return running.reshape(size_x, size_y, size_z, -1)

def weight_taps(padded, grad_out, size_x, size_y, size_z):
    channels = padded.shape[-1]
    flat_grad = grad_out.reshape(-1, grad_out.shape[-1])
    pieces = []
    for step_x, step_y, step_z in TAP_OFFSETS:
        window = padded[1 + step_x:1 + step_x + size_x, 1 + step_y:1 + step_y + size_y, 1 + step_z:1 + step_z + size_z]
        pieces.append(jnp.dot(window.reshape(-1, channels).T, flat_grad, preferred_element_type=jnp.float32))
    return jnp.stack(pieces)

def stride_window(padded, step_x, step_y, step_z, size_x, size_y, size_z):
    channels = padded.shape[-1]
    return lax.slice(padded, (1 + step_x, 1 + step_y, 1 + step_z, 0), (2 + step_x + 2 * (size_x - 1), 2 + step_y + 2 * (size_y - 1), 2 + step_z + 2 * (size_z - 1), channels), (2, 2, 2, 1))

def stride_conv(padded, weight, size_x, size_y, size_z):
    channels = padded.shape[-1]
    running = jnp.zeros((size_x * size_y * size_z, weight.shape[2]), jnp.float32)
    for tap_index, (step_x, step_y, step_z) in enumerate(TAP_OFFSETS):
        window = stride_window(padded, step_x, step_y, step_z, size_x, size_y, size_z)
        running = running + jnp.dot(window.reshape(-1, channels), weight[tap_index], preferred_element_type=jnp.float32)
    return running.reshape(size_x, size_y, size_z, -1)

def stride_weight(padded, grad_out, size_x, size_y, size_z):
    channels = padded.shape[-1]
    flat_grad = grad_out.reshape(-1, grad_out.shape[-1])
    pieces = []
    for step_x, step_y, step_z in TAP_OFFSETS:
        window = stride_window(padded, step_x, step_y, step_z, size_x, size_y, size_z)
        pieces.append(jnp.dot(window.reshape(-1, channels).T, flat_grad, preferred_element_type=jnp.float32))
    return jnp.stack(pieces)

def fine_from_coarse(padded, weight, size_x, size_y, size_z):
    channels = padded.shape[-1]
    flipped = jnp.swapaxes(weight, 1, 2)
    blocks = []
    for parity_x in (0, 1):
        for parity_y in (0, 1):
            for parity_z in (0, 1):
                running = jnp.zeros((size_x * size_y * size_z, weight.shape[1]), jnp.float32)
                for step_x, shift_x in PARITY_TERMS[parity_x]:
                    for step_y, shift_y in PARITY_TERMS[parity_y]:
                        for step_z, shift_z in PARITY_TERMS[parity_z]:
                            tap_index = (step_x + 1) * 9 + (step_y + 1) * 3 + (step_z + 1)
                            window = padded[shift_x:shift_x + size_x, shift_y:shift_y + size_y, shift_z:shift_z + size_z]
                            running = running + jnp.dot(window.reshape(-1, channels), flipped[tap_index], preferred_element_type=jnp.float32)
                blocks.append(running.reshape(size_x, size_y, size_z, -1))
    stacked = jnp.stack(blocks).reshape(2, 2, 2, size_x, size_y, size_z, -1)
    return jnp.transpose(stacked, (3, 0, 4, 1, 5, 2, 6)).reshape(2 * size_x, 2 * size_y, 2 * size_z, -1)

def reference(voxels, occupancy, conv_weight, conv_bias, down_weight, down_cotangent):
    size_x, size_y, size_z, channels = voxels.shape
    half_x, half_y, half_z = (size_x // 2, size_y // 2, size_z // 2)
    occupied = occupancy.astype(jnp.float32)[..., None]
    masked = (voxels.astype(jnp.float32) * occupied).astype(jnp.bfloat16)
    padded_in = jnp.pad(masked, ((1, 1), (1, 1), (1, 1), (0, 0)))
    preact = conv_same(padded_in, conv_weight, size_x, size_y, size_z) + conv_bias
    summed = (masked.astype(jnp.float32) + jax.nn.silu(preact) * occupied).astype(jnp.bfloat16)
    coarse_live = occupancy.reshape(half_x, 2, half_y, 2, half_z, 2).max(axis=(1, 3, 5)).astype(jnp.float32)[..., None]
    stride_in = jnp.pad(summed, ((1, 0), (1, 0), (1, 0), (0, 0)))
    down = (stride_conv(stride_in, down_weight, half_x, half_y, half_z) * coarse_live).astype(jnp.bfloat16)
    grad_coarse = (down_cotangent.astype(jnp.float32) * coarse_live).astype(jnp.bfloat16)
    grad_stride = stride_weight(stride_in, grad_coarse, half_x, half_y, half_z)
    coarse_pad = jnp.pad(grad_coarse, ((0, 1), (0, 1), (0, 1), (0, 0)))
    grad_sum = fine_from_coarse(coarse_pad, down_weight, half_x, half_y, half_z)
    sigmoid_val = jax.nn.sigmoid(preact)
    grad_pre = (grad_sum * occupied * sigmoid_val * (1.0 + preact * (1.0 - sigmoid_val))).astype(jnp.bfloat16)
    grad_bias = lax.optimization_barrier(jnp.sum(grad_pre.astype(jnp.float32), axis=(0, 1, 2)))
    grad_conv = weight_taps(padded_in, grad_pre, size_x, size_y, size_z)
    grad_padded = jnp.pad(grad_pre, ((1, 1), (1, 1), (1, 1), (0, 0)))
    back_weight = jnp.swapaxes(conv_weight[::-1], 1, 2)
    grad_in = grad_sum + conv_same(grad_padded, back_weight, size_x, size_y, size_z)
    grad_voxels = (grad_in * occupied).astype(jnp.bfloat16)
    factor = 1.0 / math.sqrt(size_x * size_y * size_z)
    return (down, grad_voxels, grad_conv * factor, grad_bias * factor, grad_stride * factor)
```

```python
import math

import jax
import jax.numpy as jnp
from jax import lax
from jax.experimental import pallas as pl
from jax.experimental.pallas import tpu as pltpu
from jax.sharding import PartitionSpec as P

F32 = jnp.float32
BF16 = jnp.bfloat16
MESH = pl.DeviceIdType.MESH

C = 96
LANES = 128
TAPS = 27
TILE = 8
HALF = 4
DEEP = 8
K_ALL = TAPS * LANES
ROWS = 2048
NX, NY, NZ = 4, 8, 8
TAP_OFFSETS = [(a, b, e) for a in (-1, 0, 1) for b in (-1, 0, 1) for e in (-1, 0, 1)]

SIDES = [(-1, 0), (1, 0), (0, -1), (0, 1), (-1, -1), (-1, 1), (1, -1), (1, 1)]
SIDE_ROWS = [160 if 0 in side else 48 for side in SIDES]
SIDE_AT = [sum(SIDE_ROWS[:i]) for i in range(8)]
HALO_ROWS = sum(SIDE_ROWS)

PIECES = [
    (0, 1, 8, 1, 8),
    (512, 0, 1, 0, 10),
    (592, 9, 1, 0, 10),
    (672, 1, 8, 0, 1),
    (736, 1, 8, 9, 1),
]


def edge(step, length, width):
    return {-1: (0, width), 0: (0, length), 1: (length - width, width)}[step]


def landing(step, length, width):
    return {-1: (0, width), 0: (width, length), 1: (width + length, width)}[step]


def dot(left, right):
    return lax.dot_general(left, right, (((1,), (0,)), ((), ())), preferred_element_type=F32)


def dot_nt(left, right):
    return lax.dot_general(left, right, (((1,), (1,)), ((), ())), preferred_element_type=F32)


def iota(shape, dim):
    return lax.broadcasted_iota(jnp.int32, shape, dim)


def z_shifts(value):
    columns = value.shape[0]
    level = iota((columns, DEEP, LANES), 1)
    below = jnp.where(level == 0, 0.0, pltpu.roll(value, 1, 1))
    above = jnp.where(level == DEEP - 1, 0.0, pltpu.roll(value, DEEP - 1, 1))
    return below, value, above


def store_shifts(ref, value, at_x, size_x, at_y, size_y):
    for k, shifted in enumerate(z_shifts(value.reshape(size_x * size_y, DEEP, LANES))):
        ref[k, at_x : at_x + size_x, at_y : at_y + size_y] = shifted.reshape(
            size_x, size_y, DEEP, LANES
        )


def dense_tiles(acc, extra):
    lane = iota((C, LANES), 1)
    tap = lambda t: acc[:, t * LANES : (t + 1) * LANES]
    tiles = []
    for group in range(7):
        first = 4 * group
        one = pltpu.roll(tap(first + 1), 96, 1)
        two = pltpu.roll(tap(first + 2), 64, 1)
        tiles.append(jnp.where(lane < 96, tap(first), one))
        tiles.append(jnp.where(lane < 64, one, two))
        if group < 6:
            three = pltpu.roll(tap(first + 3), 32, 1)
        else:
            three = jnp.where(lane == 32, pltpu.roll(extra, 64, 1), 0.0)
        tiles.append(jnp.where(lane < 32, two, three))
    return tiles


def main_kernel(
    vox_ref, occ_ref, cw_ref, bias_ref, dw_ref, cot_ref,
    fin_ref, down_ref, gv_ref,
    hs, hr, a3, c3, gs10, s3, g3, pre, p1, p2, ps, wf, wb, df, db, cl,
    part, rc, xs, xr, ys, yr, zs, zr, zg,
    h_send, h_recv, c_send, c_recv, x_send, x_recv, y_send, y_recv, z_send, z_recv,
    zg_send, zg_recv, yg_send, yg_recv, xg_send, xg_recv, cg_send, cg_recv,
):
    gx = lax.axis_index("gx")
    gy = lax.axis_index("gy")
    n_gx = lax.axis_size("gx")
    n_gy = lax.axis_size("gy")
    px, pz = gx // NZ, gx % NZ
    py, core = gy // 2, gy % 2
    sibling = (gx, gy + 1 - 2 * core)
    side_peer = [((gx + sx + n_gx) % n_gx, (gy + sy + n_gy) % n_gy) for sx, sy in SIDES]
    x_peer = [(((px + k) % NX) * NZ + pz, gy) for k in range(NX)]
    y_peer = [(gx, ((py + k) % NY) * 2 + core) for k in range(NY)]
    z_peer = [(px * NZ + (pz + k) % NZ, gy) for k in range(NZ)]

    def chosen(first, second):
        return tuple(i + core * (j - i) for i, j in zip(first, second))

    near = [chosen(y_peer[k], z_peer[k]) for k in range(8)]
    far = [chosen(z_peer[k], y_peer[k]) for k in range(8)]
    i_near = py + core * (pz - py)
    i_far = pz + core * (py - pz)

    barrier = pltpu.get_barrier_semaphore()
    greeted = side_peer + [sibling] + x_peer[1:] + y_peer[1:] + z_peer[1:]
    for peer in greeted:
        pl.semaphore_signal(barrier, inc=1, device_id=peer, device_id_type=MESH)

    def remote(src, dst, send, recv, peer):
        return pltpu.make_async_remote_copy(
            src_ref=src, dst_ref=dst, send_sem=send, recv_sem=recv, device_id=peer,
            device_id_type=MESH,
        )

    spread = (iota((512, 64), 0) // DEEP == iota((512, 64), 1)).astype(BF16)
    by_column = dot(spread, occ_ref[...].astype(F32).astype(BF16))
    own_level = iota((512, DEEP), 0) % DEEP == iota((512, DEEP), 1)
    picked = jnp.where(own_level, by_column, 0.0).astype(BF16)
    live = dot(picked, jnp.ones((DEEP, LANES), BF16))
    widen = (iota((C, LANES), 0) == iota((C, LANES), 1)).astype(BF16)
    lane512 = iota((512, LANES), 1)
    masked = jnp.where(lane512 == C, live, dot(vox_ref[...], widen) * live)
    masked = masked.reshape(TILE, TILE, DEEP, LANES)
    pairs = live.reshape(HALF, 2, HALF, 2, DEEP, LANES)
    most = jnp.maximum(
        jnp.maximum(pairs[:, 0, :, 0], pairs[:, 0, :, 1]),
        jnp.maximum(pairs[:, 1, :, 0], pairs[:, 1, :, 1]),
    ).reshape(HALF * HALF, DEEP, LANES)
    coarse_live = jnp.maximum(most, pltpu.roll(most, DEEP - 1, 1)).reshape(128, LANES)
    cl[...] = coarse_live
    upward = (iota((128, 64), 0) == 2 * iota((128, 64), 1)).astype(BF16)
    cot = (dot(upward, dot(cot_ref[...], widen).astype(BF16)) * coarse_live).reshape(
        HALF, HALF, DEEP, LANES
    )

    for i, (sx, sy) in enumerate(SIDES):
        x0, wx = edge(sx, TILE, 2)
        y0, wy = edge(sy, TILE, 2)
        rows = wx * wy * DEEP
        at = SIDE_AT[i]
        hs[at : at + rows, :] = (
            masked[x0 : x0 + wx, y0 : y0 + wy].reshape(rows, LANES).astype(BF16)
        )
        x0, wx = edge(sx, HALF, 1)
        y0, wy = edge(sy, HALF, 1)
        more = wx * wy * DEEP
        block = cot[x0 : x0 + wx, y0 : y0 + wy].reshape(more, LANES)
        if more < 16:
            block = jnp.concatenate([block, jnp.zeros((16 - more, LANES), F32)], 0)
        hs[at + rows : at + SIDE_ROWS[i], :] = block.astype(BF16)

    pl.semaphore_wait(barrier, len(greeted))
    halo = []
    for i, (sx, sy) in enumerate(SIDES):
        there = SIDES.index((-sx, -sy))
        mine = pl.ds(SIDE_AT[i], SIDE_ROWS[i])
        theirs = pl.ds(SIDE_AT[there], SIDE_ROWS[i])
        copy = remote(hs.at[mine], hr.at[theirs], h_send.at[i], h_recv.at[there], side_peer[i])
        copy.start()
        halo.append(copy)

    store_shifts(a3, masked, 2, TILE, 2, TILE)
    store_shifts(c3, cot, 1, HALF, 1, HALF)
    for ref in (wf, wb, df, db):
        ref[...] = jnp.zeros(ref.shape, BF16)
    for t in range(TAPS):
        for source, plain, turned in ((cw_ref, wf, wb), (dw_ref, df, db)):
            block = source[t]
            plain[t * LANES : t * LANES + C, 0:C] = block
            turned[0:C, t * LANES : t * LANES + C] = block
    for w in (0, 1):
        part[w, 2016:2048, :] = jnp.zeros((32, LANES), BF16)

    for copy in halo:
        copy.wait()
    for i, (sx, sy) in enumerate(SIDES):
        inside = 1.0
        for step, at, size in ((sx, gx, n_gx), (sy, gy, n_gy)):
            if step:
                inside = inside * jnp.where(at == (0 if step < 0 else size - 1), 0.0, 1.0)
        at = SIDE_AT[i]
        x0, wx = landing(sx, TILE, 2)
        y0, wy = landing(sy, TILE, 2)
        rows = wx * wy * DEEP
        store_shifts(a3, hr[at : at + rows, :].astype(F32) * inside, x0, wx, y0, wy)
        x0, wx = landing(sx, HALF, 1)
        y0, wy = landing(sy, HALF, 1)
        more = wx * wy * DEEP
        block = hr[at + rows : at + SIDE_ROWS[i], :].astype(F32)[:more] * inside
        store_shifts(c3, block, x0, wx, y0, wy)

    for t, (a, b, e) in enumerate(TAP_OFFSETS):
        lanes = slice(t * LANES, (t + 1) * LANES)
        for row, x0, wx, y0, wy in PIECES:
            x1, y1 = x0 + 1 + a, y0 + 1 + b
            rows = wx * wy * DEEP
            window = a3[e + 1, x1 : x1 + wx, y1 : y1 + wy]
            p1[row : row + rows, lanes] = window.reshape(rows, LANES).astype(BF16)
    pre[...] = dot(p1[...], wf[...]) + bias_ref[...]

    for parity_x in (0, 1):
        for parity_y in (0, 1):
            total = None
            for a in ((-1, 1) if parity_x else (0,)):
                for b in ((-1, 1) if parity_y else (0,)):
                    x0 = 0 if a == 1 else 1
                    y0 = 0 if b == 1 else 1
                    windows = [
                        c3[1 - e, x0 : x0 + 5, y0 : y0 + 5].reshape(200, LANES).astype(BF16)
                        for e in (-1, 0, 1)
                    ]
                    t = 9 * (a + 1) + 3 * (b + 1)
                    term = dot_nt(
                        jnp.concatenate(windows, 1), db[:, t * LANES : (t + 3) * LANES]
                    )
                    total = term if total is None else total + term
            gs10[:, 1 - parity_x, :, 1 - parity_y] = total.reshape(5, 5, DEEP, LANES)

    pick_live = (iota((LANES, LANES), 0) == C).astype(BF16)
    ten = gs10.reshape(10, 10, DEEP, LANES)
    for row, x0, wx, y0, wy in PIECES:
        rows = wx * wy * DEEP
        value = pre[row : row + rows, :]
        feature = p1[row : row + rows, 13 * LANES : 14 * LANES]
        alive = dot(feature, pick_live)
        gate = 1.0 / (1.0 + jnp.exp(-value))
        summed = (feature.astype(F32) + alive * (value * gate)).astype(BF16).astype(F32)
        grad_sum = ten[x0 : x0 + wx, y0 : y0 + wy].reshape(rows, LANES)
        grad_pre = grad_sum * alive * gate * (1.0 + value * (1.0 - gate))
        store_shifts(s3, summed, x0, wx, y0, wy)
        store_shifts(g3, grad_pre.astype(BF16).astype(F32), x0, wx, y0, wy)

    six = s3.reshape(3, 5, 2, 5, 2, DEEP, LANES)
    for t, (a, b, e) in enumerate(TAP_OFFSETS):
        i0, si = (a + 1) // 2, (a + 1) % 2
        j0, sj = (b + 1) // 2, (b + 1) % 2
        window = six[e + 1, i0 : i0 + 4, si, j0 : j0 + 4, sj]
        ps[:, t * LANES : (t + 1) * LANES] = window.reshape(128, LANES).astype(BF16)
    cot_turned = c3[1, 1:5, 1:5].reshape(128, LANES).T[0:C].astype(BF16)
    acc = dot(cot_turned, ps[...])
    for j, tile in enumerate(dense_tiles(acc, jnp.zeros((C, LANES), F32))):
        part[1, j * C : (j + 1) * C, :] = tile.astype(BF16)

    order = (2, 1, 3, 0)
    chunk = [pl.ds(pl.multiple_of(((px + k) % NX) * 512, 512), 512) for k in range(NX)]
    core_copies = [
        remote(part.at[1 - core, chunk[k]], rc.at[chunk[k]], c_send.at[k], c_recv.at[k], sibling)
        for k in range(NX)
    ]

    @pl.when(core == 0)
    def _():
        for k in order:
            core_copies[k].start()

    pre_turned = g3[1, 1:9, 1:9].reshape(512, LANES).T[0:C].astype(BF16)
    acc = dot(pre_turned, p1[0:512, :])
    for j, tile in enumerate(dense_tiles(acc, acc[:, 13 * LANES : 14 * LANES])):
        part[0, j * C : (j + 1) * C, :] = tile.astype(BF16)

    @pl.when(core == 1)
    def _():
        for k in order:
            core_copies[k].start()

    downward = (iota((64, 128), 1) == 2 * iota((64, 128), 0)).astype(BF16)
    coarse = (dot(ps[...], df[...]) * cl[...]).astype(BF16)
    down_ref[...] = dot(downward, coarse).astype(BF16)

    x_copies = []
    for k in order:
        core_copies[k].wait()
        both = part[core, chunk[k]].astype(F32) + rc[chunk[k]].astype(F32)
        xs[k] = both.astype(BF16)
        if k:
            copy = remote(xs.at[k], xr.at[k], x_send.at[k], x_recv.at[k], x_peer[k])
            copy.start()
            x_copies.append(copy)

    for t, (a, b, e) in enumerate(TAP_OFFSETS):
        window = g3[1 - e, 1 - a : 9 - a, 1 - b : 9 - b]
        p2[:, t * LANES : (t + 1) * LANES] = window.reshape(512, LANES).astype(BF16)
    grad_in = ten[1:9, 1:9].reshape(512, LANES) + dot_nt(p2[...], wb[...])
    alive = dot(p1[0:512, 13 * LANES : 14 * LANES], pick_live)
    gv_ref[...] = (grad_in * alive).astype(BF16)

    for copy in x_copies:
        copy.wait()
    ys[...] = (
        xs[0].astype(F32) + xr[1].astype(F32) + xr[2].astype(F32) + xr[3].astype(F32)
    ).astype(BF16).reshape(8, 64, LANES)
    copies = []
    for k in (4, 3, 5, 2, 6, 1, 7):
        block = ys.at[(i_near + k) % 8]
        copies.append(remote(block, yr.at[k], y_send.at[k], y_recv.at[k], near[k]))
        copies[-1].start()
    for copy in copies:
        copy.wait()
    total = ys[i_near].astype(F32)
    for k in range(1, 8):
        total = total + yr[k].astype(F32)
    zs[...] = total.reshape(8, 8, LANES)
    copies = []
    for k in (4, 3, 5, 2, 6, 1, 7):
        block = zs.at[(i_far + k) % 8]
        copies.append(remote(block, zr.at[k], z_send.at[k], z_recv.at[k], far[k]))
        copies[-1].start()
    for copy in copies:
        copy.wait()
    total = zs[i_far]
    for k in range(1, 8):
        total = total + zr[k]

    zg[i_far] = total
    copies = []
    for k in (4, 3, 5, 2, 6, 1, 7):
        block = zg.at[i_far]
        copies.append(remote(block, block, zg_send.at[k], zg_recv.at[k], far[k]))
        copies[-1].start()
    for copy in copies:
        copy.wait()
    own = pl.ds(pl.multiple_of(px * 512 + i_near * 64, 64), 64)
    fin_ref[core, own] = zg[...].reshape(64, LANES).astype(BF16)
    copies = []
    for k in (4, 3, 5, 2, 6, 1, 7):
        block = fin_ref.at[core, own]
        copies.append(remote(block, block, yg_send.at[k], yg_recv.at[k], near[k]))
        copies[-1].start()
    for copy in copies:
        copy.wait()
    copies = {}
    for k in (2, 1, 3):
        block = fin_ref.at[core, chunk[0]]
        copies[k] = remote(block, block, xg_send.at[k], xg_recv.at[k], x_peer[k])
        copies[k].start()
    last = []
    for k in (0, 1, 3, 2):
        if k:
            copies[k].wait()
        block = fin_ref.at[core, chunk[-k % NX]]
        last.append(remote(block, block, cg_send.at[k], cg_recv.at[k], sibling))
        last[-1].start()
    for copy in last:
        copy.wait()


def finish_kernel(factor, fin_ref, down_in, gv_in, down_ref, gv_ref, gc_ref, gb_ref, gd_ref):
    down_ref[...] = down_in[:, 0:C]
    gv_ref[...] = gv_in[:, 0:C]
    lane = iota((C, LANES), 1)
    for w, out in ((0, gc_ref), (1, gd_ref)):
        for group in range(7):
            first, second, third = (
                fin_ref[w, (3 * group + i) * C : (3 * group + i + 1) * C, :].astype(F32) * factor
                for i in range(3)
            )
            taps = [
                first,
                pltpu.roll(jnp.where(lane >= 96, first, second), 32, 1),
                pltpu.roll(jnp.where(lane >= 64, second, third), 64, 1),
                pltpu.roll(third, 96, 1),
            ]
            for i in range(4 if group < 6 else 3):
                out[4 * group + i] = taps[i].T[0:C]
        if w == 0:
            gb_ref[...] = third.T[32:33]


def on_device(voxels, occupancy, conv_weight, conv_bias, down_weight, down_cotangent):
    vmem = pl.BlockSpec(memory_space=pltpu.VMEM)
    bias = jnp.pad(conv_bias, (0, LANES - C)).reshape(1, LANES)
    scratch = [
        ((HALO_ROWS, LANES), BF16),
        ((HALO_ROWS, LANES), BF16),
        ((3, 12, 12, DEEP, LANES), F32),
        ((3, 6, 6, DEEP, LANES), F32),
        ((5, 2, 5, 2, DEEP, LANES), F32),
        ((3, 10, 10, DEEP, LANES), F32),
        ((3, 10, 10, DEEP, LANES), F32),
        ((800, LANES), F32),
        ((800, K_ALL), BF16),
        ((512, K_ALL), BF16),
        ((128, K_ALL), BF16),
        ((K_ALL, LANES), BF16),
        ((LANES, K_ALL), BF16),
        ((K_ALL, LANES), BF16),
        ((LANES, K_ALL), BF16),
        ((128, LANES), F32),
        ((2, ROWS, LANES), BF16),
        ((ROWS, LANES), BF16),
        ((4, 512, LANES), BF16),
        ((4, 512, LANES), BF16),
        ((8, 64, LANES), BF16),
        ((8, 64, LANES), BF16),
        ((8, 8, LANES), F32),
        ((8, 8, LANES), F32),
        ((8, 8, LANES), F32),
    ]
    semaphores = [8, 8, 4, 4, 4, 4, 8, 8, 8, 8, 8, 8, 8, 8, 4, 4, 4, 4]
    fin, down, grad_voxels = pl.pallas_call(
        main_kernel,
        out_shape=(
            jax.ShapeDtypeStruct((2, ROWS, LANES), BF16),
            jax.ShapeDtypeStruct((64, LANES), BF16),
            jax.ShapeDtypeStruct((512, LANES), BF16),
        ),
        in_specs=[vmem] * 6,
        out_specs=(vmem, vmem, vmem),
        scratch_shapes=[pltpu.VMEM(shape, dtype) for shape, dtype in scratch]
        + [pltpu.SemaphoreType.DMA((n,)) for n in semaphores],
        compiler_params=pltpu.CompilerParams(
            collective_id=0, has_side_effects=True, vmem_limit_bytes=56 * 1024 * 1024
        ),
    )(
        voxels.reshape(512, C),
        occupancy.reshape(64, DEEP),
        conv_weight,
        bias,
        down_weight,
        down_cotangent.reshape(64, C),
    )
    cells = voxels.shape[0] * lax.axis_size("gx") * voxels.shape[1] * lax.axis_size("gy") * DEEP
    factor = 1.0 / math.sqrt(cells)
    down, grad_voxels, grad_conv, grad_bias, grad_down = pl.pallas_call(
        lambda *refs: finish_kernel(factor, *refs),
        out_shape=(
            jax.ShapeDtypeStruct((64, C), BF16),
            jax.ShapeDtypeStruct((512, C), BF16),
            jax.ShapeDtypeStruct((TAPS, C, C), F32),
            jax.ShapeDtypeStruct((1, C), F32),
            jax.ShapeDtypeStruct((TAPS, C, C), F32),
        ),
        in_specs=[vmem] * 3,
        out_specs=(vmem,) * 5,
        compiler_params=pltpu.CompilerParams(vmem_limit_bytes=32 * 1024 * 1024),
    )(fin, down, grad_voxels)
    return (
        down.reshape(down_cotangent.shape),
        grad_voxels.reshape(voxels.shape),
        grad_conv,
        grad_bias.reshape(C),
        grad_down,
    )


def solution(mesh):
    tile = P("gx", "gy", None, None)
    return jax.shard_map(
        on_device,
        mesh=mesh,
        in_specs=(tile, P("gx", "gy", None), P(), P(), P(), tile),
        out_specs=(tile, tile, P(), P(), P()),
        check_vma=False,
    )
```

```python
import math

import jax
import jax.numpy as jnp
from jax import lax
from jax.experimental import pallas as pl
from jax.experimental.pallas import tpu as pltpu
from jax.sharding import PartitionSpec as P

F32 = jnp.float32
BF16 = jnp.bfloat16
MESH = pl.DeviceIdType.MESH

C = 96
LANES = 128
TAPS = 27
TILE = 8
HALF = 4
DEEP = 8
K_ALL = TAPS * LANES
ROWS = 2048
NX, NY, NZ = 4, 8, 8
TAP_OFFSETS = [(a, b, e) for a in (-1, 0, 1) for b in (-1, 0, 1) for e in (-1, 0, 1)]

SIDES = [(-1, 0), (1, 0), (0, -1), (0, 1), (-1, -1), (-1, 1), (1, -1), (1, 1)]
SIDE_ROWS = [160 if 0 in side else 48 for side in SIDES]
SIDE_AT = [sum(SIDE_ROWS[:i]) for i in range(8)]
HALO_ROWS = sum(SIDE_ROWS)

PIECES = [
    (0, 1, 8, 1, 8),
    (512, 0, 1, 0, 10),
    (592, 9, 1, 0, 10),
    (672, 1, 8, 0, 1),
    (736, 1, 8, 9, 1),
]


def edge(step, length, width):
    return {-1: (0, width), 0: (0, length), 1: (length - width, width)}[step]


def landing(step, length, width):
    return {-1: (0, width), 0: (width, length), 1: (width + length, width)}[step]


def dot(left, right):
    return lax.dot_general(left, right, (((1,), (0,)), ((), ())), preferred_element_type=F32)


def dot_nt(left, right):
    return lax.dot_general(left, right, (((1,), (1,)), ((), ())), preferred_element_type=F32)


def iota(shape, dim):
    return lax.broadcasted_iota(jnp.int32, shape, dim)


def z_shifts(value):
    columns = value.shape[0]
    level = iota((columns, DEEP, LANES), 1)
    below = jnp.where(level == 0, 0.0, pltpu.roll(value, 1, 1))
    above = jnp.where(level == DEEP - 1, 0.0, pltpu.roll(value, DEEP - 1, 1))
    return below, value, above


def store_shifts(ref, value, at_x, size_x, at_y, size_y):
    for k, shifted in enumerate(z_shifts(value.reshape(size_x * size_y, DEEP, LANES))):
        ref[k, at_x : at_x + size_x, at_y : at_y + size_y] = shifted.reshape(
            size_x, size_y, DEEP, LANES
        )


def dense_tiles(acc, extra):
    lane = iota((C, LANES), 1)
    tap = lambda t: acc[:, t * LANES : (t + 1) * LANES]
    tiles = []
    for group in range(7):
        first = 4 * group
        one = pltpu.roll(tap(first + 1), 96, 1)
        two = pltpu.roll(tap(first + 2), 64, 1)
        tiles.append(jnp.where(lane < 96, tap(first), one))
        tiles.append(jnp.where(lane < 64, one, two))
        if group < 6:
            three = pltpu.roll(tap(first + 3), 32, 1)
        else:
            three = jnp.where(lane == 32, pltpu.roll(extra, 64, 1), 0.0)
        tiles.append(jnp.where(lane < 32, two, three))
    return tiles


def main_kernel(
    vox_hbm, occ_hbm, cw_hbm, bias_hbm, dw_hbm, cot_hbm,
    fin_ref, down_ref, gv_ref,
    vox_ref, occ_ref, cw_ref, bias_ref, dw_ref, cot_ref, bias_row,
    hs, hr, a3, c3, gs10, s3, g3, pre, p1, p2, ps, wf, wb, df, db, cl,
    part, rc, xa, xa_in, nb, nb_in, na, na_in, xb, xb_in, far_in,
    in_sem, h_send, h_recv, c_send, c_recv, xa_send, xa_recv, nb_send, nb_recv,
    na_send, na_recv, xb_send, xb_recv, far_send, far_recv,
    gna_send, gna_recv, gxb_send, gxb_recv, gnb_send, gnb_recv, gxa_send, gxa_recv,
    gc_send, gc_recv,
):
    gx = lax.axis_index("gx")
    gy = lax.axis_index("gy")
    n_gx = lax.axis_size("gx")
    n_gy = lax.axis_size("gy")
    px, pz = gx // NZ, gx % NZ
    py, core = gy // 2, gy % 2
    sibling = (gx, gy + 1 - 2 * core)
    side_peer = [((gx + sx + n_gx) % n_gx, (gy + sy + n_gy) % n_gy) for sx, sy in SIDES]
    x_peer = [(((px + k) % NX) * NZ + pz, gy) for k in range(NX)]
    y_peer = [(gx, ((py + k) % NY) * 2 + core) for k in range(NY)]
    z_peer = [(px * NZ + (pz + k) % NZ, gy) for k in range(NZ)]

    def chosen(first, second):
        return tuple(i + core * (j - i) for i, j in zip(first, second))

    near = [chosen(y_peer[k], z_peer[k]) for k in range(8)]
    far = [chosen(z_peer[k], y_peer[k]) for k in range(8)]
    i_near = py + core * (pz - py)
    i_far = pz + core * (py - pz)

    barrier = pltpu.get_barrier_semaphore()
    greeted = side_peer + [sibling] + x_peer[1:] + y_peer[1:] + z_peer[1:]
    for peer in greeted:
        pl.semaphore_signal(barrier, inc=1, device_id=peer, device_id_type=MESH)

    loads = [
        pltpu.make_async_copy(src, dst, in_sem.at[i])
        for i, (src, dst) in enumerate(
            (
                (occ_hbm, occ_ref),
                (vox_hbm, vox_ref),
                (cot_hbm, cot_ref),
                (cw_hbm, cw_ref),
                (dw_hbm, dw_ref),
                (bias_hbm, bias_ref),
            )
        )
    ]
    for load in loads:
        load.start()

    def remote(src, dst, send, recv, peer):
        return pltpu.make_async_remote_copy(
            src_ref=src, dst_ref=dst, send_sem=send, recv_sem=recv, device_id=peer,
            device_id_type=MESH,
        )

    for load in loads[:3]:
        load.wait()

    spread = (iota((512, 64), 0) // DEEP == iota((512, 64), 1)).astype(BF16)
    by_column = dot(spread, occ_ref[...].astype(F32).astype(BF16))
    own_level = iota((512, DEEP), 0) % DEEP == iota((512, DEEP), 1)
    picked = jnp.where(own_level, by_column, 0.0).astype(BF16)
    live = dot(picked, jnp.ones((DEEP, LANES), BF16))
    widen = (iota((C, LANES), 0) == iota((C, LANES), 1)).astype(BF16)
    lane512 = iota((512, LANES), 1)
    masked = jnp.where(lane512 == C, live, dot(vox_ref[...], widen) * live)
    masked = masked.reshape(TILE, TILE, DEEP, LANES)
    pairs = live.reshape(HALF, 2, HALF, 2, DEEP, LANES)
    most = jnp.maximum(
        jnp.maximum(pairs[:, 0, :, 0], pairs[:, 0, :, 1]),
        jnp.maximum(pairs[:, 1, :, 0], pairs[:, 1, :, 1]),
    ).reshape(HALF * HALF, DEEP, LANES)
    coarse_live = jnp.maximum(most, pltpu.roll(most, DEEP - 1, 1)).reshape(128, LANES)
    cl[...] = coarse_live
    upward = (iota((128, 64), 0) == 2 * iota((128, 64), 1)).astype(BF16)
    cot = (dot(upward, dot(cot_ref[...], widen).astype(BF16)) * coarse_live).reshape(
        HALF, HALF, DEEP, LANES
    )

    for i, (sx, sy) in enumerate(SIDES):
        x0, wx = edge(sx, TILE, 2)
        y0, wy = edge(sy, TILE, 2)
        rows = wx * wy * DEEP
        at = SIDE_AT[i]
        hs[at : at + rows, :] = (
            masked[x0 : x0 + wx, y0 : y0 + wy].reshape(rows, LANES).astype(BF16)
        )
        x0, wx = edge(sx, HALF, 1)
        y0, wy = edge(sy, HALF, 1)
        more = wx * wy * DEEP
        block = cot[x0 : x0 + wx, y0 : y0 + wy].reshape(more, LANES)
        if more < 16:
            block = jnp.concatenate([block, jnp.zeros((16 - more, LANES), F32)], 0)
        hs[at + rows : at + SIDE_ROWS[i], :] = block.astype(BF16)

    pl.semaphore_wait(barrier, len(greeted))
    halo = []
    for i, (sx, sy) in enumerate(SIDES):
        there = SIDES.index((-sx, -sy))
        mine = pl.ds(SIDE_AT[i], SIDE_ROWS[i])
        theirs = pl.ds(SIDE_AT[there], SIDE_ROWS[i])
        copy = remote(hs.at[mine], hr.at[theirs], h_send.at[i], h_recv.at[there], side_peer[i])
        copy.start()
        halo.append(copy)

    store_shifts(a3, masked, 2, TILE, 2, TILE)
    store_shifts(c3, cot, 1, HALF, 1, HALF)
    for ref in (wf, wb, df, db):
        ref[...] = jnp.zeros(ref.shape, BF16)
    bias_row[...] = jnp.zeros((1, LANES), F32)
    for load in loads[3:]:
        load.wait()
    bias_row[:, 0:C] = bias_ref[...]
    for t in range(TAPS):
        for source, plain, turned in ((cw_ref, wf, wb), (dw_ref, df, db)):
            block = source[t]
            plain[t * LANES : t * LANES + C, 0:C] = block
            turned[0:C, t * LANES : t * LANES + C] = block
    for w in (0, 1):
        part[w, 2016:2048, :] = jnp.zeros((32, LANES), BF16)

    for copy in halo:
        copy.wait()
    for i, (sx, sy) in enumerate(SIDES):
        inside = 1.0
        for step, at, size in ((sx, gx, n_gx), (sy, gy, n_gy)):
            if step:
                inside = inside * jnp.where(at == (0 if step < 0 else size - 1), 0.0, 1.0)
        at = SIDE_AT[i]
        x0, wx = landing(sx, TILE, 2)
        y0, wy = landing(sy, TILE, 2)
        rows = wx * wy * DEEP
        store_shifts(a3, hr[at : at + rows, :].astype(F32) * inside, x0, wx, y0, wy)
        x0, wx = landing(sx, HALF, 1)
        y0, wy = landing(sy, HALF, 1)
        more = wx * wy * DEEP
        block = hr[at + rows : at + SIDE_ROWS[i], :].astype(F32)[:more] * inside
        store_shifts(c3, block, x0, wx, y0, wy)

    for t, (a, b, e) in enumerate(TAP_OFFSETS):
        lanes = slice(t * LANES, (t + 1) * LANES)
        for row, x0, wx, y0, wy in PIECES:
            x1, y1 = x0 + 1 + a, y0 + 1 + b
            rows = wx * wy * DEEP
            window = a3[e + 1, x1 : x1 + wx, y1 : y1 + wy]
            p1[row : row + rows, lanes] = window.reshape(rows, LANES).astype(BF16)
    pre[...] = dot(p1[...], wf[...]) + bias_row[...]

    for parity_x in (0, 1):
        for parity_y in (0, 1):
            total = None
            for a in ((-1, 1) if parity_x else (0,)):
                for b in ((-1, 1) if parity_y else (0,)):
                    x0 = 0 if a == 1 else 1
                    y0 = 0 if b == 1 else 1
                    windows = [
                        c3[1 - e, x0 : x0 + 5, y0 : y0 + 5].reshape(200, LANES).astype(BF16)
                        for e in (-1, 0, 1)
                    ]
                    t = 9 * (a + 1) + 3 * (b + 1)
                    term = dot_nt(
                        jnp.concatenate(windows, 1), db[:, t * LANES : (t + 3) * LANES]
                    )
                    total = term if total is None else total + term
            gs10[:, 1 - parity_x, :, 1 - parity_y] = total.reshape(5, 5, DEEP, LANES)

    pick_live = (iota((LANES, LANES), 0) == C).astype(BF16)
    ten = gs10.reshape(10, 10, DEEP, LANES)
    for row, x0, wx, y0, wy in PIECES:
        rows = wx * wy * DEEP
        value = pre[row : row + rows, :]
        feature = p1[row : row + rows, 13 * LANES : 14 * LANES]
        alive = dot(feature, pick_live)
        gate = 1.0 / (1.0 + jnp.exp(-value))
        summed = (feature.astype(F32) + alive * (value * gate)).astype(BF16).astype(F32)
        grad_sum = ten[x0 : x0 + wx, y0 : y0 + wy].reshape(rows, LANES)
        grad_pre = grad_sum * alive * gate * (1.0 + value * (1.0 - gate))
        store_shifts(s3, summed, x0, wx, y0, wy)
        store_shifts(g3, grad_pre.astype(BF16).astype(F32), x0, wx, y0, wy)

    six = s3.reshape(3, 5, 2, 5, 2, DEEP, LANES)
    for t, (a, b, e) in enumerate(TAP_OFFSETS):
        i0, si = (a + 1) // 2, (a + 1) % 2
        j0, sj = (b + 1) // 2, (b + 1) % 2
        window = six[e + 1, i0 : i0 + 4, si, j0 : j0 + 4, sj]
        ps[:, t * LANES : (t + 1) * LANES] = window.reshape(128, LANES).astype(BF16)
    cot_turned = c3[1, 1:5, 1:5].reshape(128, LANES).T[0:C].astype(BF16)
    acc = dot(cot_turned, ps[...])
    for j, tile in enumerate(dense_tiles(acc, jnp.zeros((C, LANES), F32))):
        part[1, j * C : (j + 1) * C, :] = tile.astype(BF16)

    rows_a = [pl.ds(pl.multiple_of(((px + k) % NX) * 256, 256), 256) for k in range(NX)]
    rows_b = [
        pl.ds(pl.multiple_of(1024 + ((i_near + k) % 8) * 128, 128), 128) for k in range(8)
    ]
    sibling_b = [
        pl.ds(pl.multiple_of(1024 + ((i_far + k) % 8) * 128, 128), 128) for k in range(8)
    ]
    order = (("a", 2), ("b", 4), ("a", 1), ("b", 3), ("b", 5), ("a", 3))
    order += (("b", 2), ("b", 6), ("a", 0), ("b", 1), ("b", 7), ("b", 0))
    core_copies = []
    for i, (which, k) in enumerate(order):
        rows = rows_a[k] if which == "a" else sibling_b[k]
        core_copies.append(
            remote(part.at[1 - core, rows], rc.at[rows], c_send.at[i], c_recv.at[i], sibling)
        )

    @pl.when(core == 0)
    def _():
        for copy in core_copies:
            copy.start()

    pre_turned = g3[1, 1:9, 1:9].reshape(512, LANES).T[0:C].astype(BF16)
    acc = dot(pre_turned, p1[0:512, :])
    for j, tile in enumerate(dense_tiles(acc, acc[:, 13 * LANES : 14 * LANES])):
        part[0, j * C : (j + 1) * C, :] = tile.astype(BF16)

    @pl.when(core == 1)
    def _():
        for copy in core_copies:
            copy.start()

    xa_copies, nb_copies = {}, {}
    for copy, (which, k) in zip(core_copies, order):
        copy.wait()
        rows = rows_a[k] if which == "a" else rows_b[k]
        both = (part[core, rows].astype(F32) + rc[rows].astype(F32)).astype(BF16)
        if which == "a":
            xa[k] = both
            if k:
                xa_copies[k] = remote(
                    xa.at[k], xa_in.at[k], xa_send.at[k], xa_recv.at[k], x_peer[k]
                )
                xa_copies[k].start()
        else:
            nb[k] = both
            if k:
                nb_copies[k] = remote(
                    nb.at[k], nb_in.at[k], nb_send.at[k], nb_recv.at[k], near[k]
                )
                nb_copies[k].start()

    downward = (iota((64, 128), 1) == 2 * iota((64, 128), 0)).astype(BF16)
    coarse = (dot(ps[...], df[...]) * cl[...]).astype(BF16)
    down_ref[...] = dot(downward, coarse).astype(BF16)[:, 0:C]

    for t, (a, b, e) in enumerate(TAP_OFFSETS):
        window = g3[1 - e, 1 - a : 9 - a, 1 - b : 9 - b]
        p2[:, t * LANES : (t + 1) * LANES] = window.reshape(512, LANES).astype(BF16)
    grad_in = ten[1:9, 1:9].reshape(512, LANES) + dot_nt(p2[...], wb[...])
    alive = dot(p1[0:512, 13 * LANES : 14 * LANES], pick_live)
    gv_ref[...] = (grad_in * alive).astype(BF16)[:, 0:C]

    far_first = (4, 3, 5, 2, 6, 1, 7)
    total = xa[0].astype(F32)
    for k in (1, 3, 2):
        xa_copies[k].wait()
        total = total + xa_in[k].astype(F32)
    na[...] = total.reshape(8, 32, LANES).astype(BF16)
    na_copies = {}
    for k in far_first:
        block = na.at[(i_near + k) % 8]
        na_copies[k] = remote(block, na_in.at[k], na_send.at[k], na_recv.at[k], near[k])
        na_copies[k].start()
    total = nb[0].astype(F32)
    for k in (1, 7, 2, 6, 3, 5, 4):
        nb_copies[k].wait()
        total = total + nb_in[k].astype(F32)
    xb[...] = total.reshape(4, 32, LANES).astype(BF16)
    xb_copies = {}
    for k in (2, 1, 3):
        block = xb.at[(px + k) % NX]
        xb_copies[k] = remote(block, xb_in.at[k], xb_send.at[k], xb_recv.at[k], x_peer[k])
        xb_copies[k].start()

    total = xb[px].astype(F32)
    for k in (1, 3, 2):
        xb_copies[k].wait()
        total = total + xb_in[k].astype(F32)
    far_in[i_far, 32:64] = total.astype(BF16)
    total = na[i_near].astype(F32)
    for k in (1, 7, 2, 6, 3, 5, 4):
        na_copies[k].wait()
        total = total + na_in[k].astype(F32)
    far_in[i_far, 0:32] = total.astype(BF16)
    copies = []
    for k in far_first:
        block = far_in.at[i_far]
        copies.append(remote(block, block, far_send.at[k], far_recv.at[k], far[k]))
        copies[-1].start()
    for copy in copies:
        copy.wait()
    total = far_in[0].astype(F32)
    for k in range(1, 8):
        total = total + far_in[k].astype(F32)
    total = total.astype(BF16)

    own_a = pl.ds(pl.multiple_of(px * 256 + i_near * 32, 32), 32)
    own_b = pl.ds(pl.multiple_of(1024 + i_near * 128 + px * 32, 32), 32)
    fin_ref[core, own_a] = total[0:32]
    fin_ref[core, own_b] = total[32:64]
    gxb_copies, gna_copies, gnb_copies, gxa_copies = {}, {}, {}, {}
    for k in (2, 1, 3):
        block = fin_ref.at[core, own_b]
        gxb_copies[k] = remote(block, block, gxb_send.at[k], gxb_recv.at[k], x_peer[k])
        gxb_copies[k].start()
    for k in far_first:
        block = fin_ref.at[core, own_a]
        gna_copies[k] = remote(block, block, gna_send.at[k], gna_recv.at[k], near[k])
        gna_copies[k].start()
    for k in (1, 3, 2):
        gxb_copies[k].wait()
    for k in far_first:
        block = fin_ref.at[core, rows_b[0]]
        gnb_copies[k] = remote(block, block, gnb_send.at[k], gnb_recv.at[k], near[k])
        gnb_copies[k].start()
    for k in (1, 7, 2, 6, 3, 5, 4):
        gna_copies[k].wait()
    for k in (2, 1, 3):
        block = fin_ref.at[core, rows_a[0]]
        gxa_copies[k] = remote(block, block, gxa_send.at[k], gxa_recv.at[k], x_peer[k])
        gxa_copies[k].start()
    last = []

    def hand_over(rows):
        i = len(last)
        block = fin_ref.at[core, rows]
        last.append(remote(block, block, gc_send.at[i], gc_recv.at[i], sibling))
        last[-1].start()

    hand_over(rows_b[0])
    hand_over(rows_a[0])
    for which, k in (
        ("b", 1), ("b", 7), ("a", 1), ("a", 3), ("b", 2), ("b", 6), ("b", 3), ("b", 5), ("a", 2),
        ("b", 4),
    ):
        if which == "a":
            gxa_copies[k].wait()
            hand_over(rows_a[-k % NX])
        else:
            gnb_copies[k].wait()
            hand_over(rows_b[-k % 8])
    for copy in last:
        copy.wait()


def finish_kernel(
    factor, fin_ref, down_in, gv_in, down_ref, gv_ref, gc_ref, gb_ref, gd_ref,
    gc, gb, gd, sem,
):
    copies = []

    def send_out(src, dst):
        copies.append(pltpu.make_async_copy(src, dst, sem.at[len(copies)]))
        copies[-1].start()

    send_out(down_in, down_ref)
    send_out(gv_in, gv_ref)
    lane = iota((C, LANES), 1)
    for w, held, out in ((1, gd, gd_ref), (0, gc, gc_ref)):
        for group in range(7):
            first, second, third = (
                fin_ref[w, (3 * group + i) * C : (3 * group + i + 1) * C, :].astype(F32) * factor
                for i in range(3)
            )
            taps = [
                first,
                pltpu.roll(jnp.where(lane >= 96, first, second), 32, 1),
                pltpu.roll(jnp.where(lane >= 64, second, third), 64, 1),
                pltpu.roll(third, 96, 1),
            ]
            count = 4 if group < 6 else 3
            for i in range(count):
                held[4 * group + i] = taps[i].T[0:C]
            block = pl.ds(4 * group, count)
            send_out(held.at[block], out.at[block])
        if w == 0:
            gb[...] = third.T[32:33]
            send_out(gb, gb_ref)
    for copy in copies:
        copy.wait()


def on_device(voxels, occupancy, conv_weight, conv_bias, down_weight, down_cotangent):
    vmem = pl.BlockSpec(memory_space=pltpu.VMEM)
    anywhere = pl.BlockSpec(memory_space=pl.ANY)
    scratch = [
        ((512, C), BF16),
        ((64, DEEP), jnp.int32),
        ((TAPS, C, C), BF16),
        ((1, C), F32),
        ((TAPS, C, C), BF16),
        ((64, C), BF16),
        ((1, LANES), F32),
        ((HALO_ROWS, LANES), BF16),
        ((HALO_ROWS, LANES), BF16),
        ((3, 12, 12, DEEP, LANES), F32),
        ((3, 6, 6, DEEP, LANES), F32),
        ((5, 2, 5, 2, DEEP, LANES), F32),
        ((3, 10, 10, DEEP, LANES), F32),
        ((3, 10, 10, DEEP, LANES), F32),
        ((800, LANES), F32),
        ((800, K_ALL), BF16),
        ((512, K_ALL), BF16),
        ((128, K_ALL), BF16),
        ((K_ALL, LANES), BF16),
        ((LANES, K_ALL), BF16),
        ((K_ALL, LANES), BF16),
        ((LANES, K_ALL), BF16),
        ((128, LANES), F32),
        ((2, ROWS, LANES), BF16),
        ((ROWS, LANES), BF16),
        ((4, 256, LANES), BF16),
        ((4, 256, LANES), BF16),
        ((8, 128, LANES), BF16),
        ((8, 128, LANES), BF16),
        ((8, 32, LANES), BF16),
        ((8, 32, LANES), BF16),
        ((4, 32, LANES), BF16),
        ((4, 32, LANES), BF16),
        ((8, 64, LANES), BF16),
    ]
    semaphores = [6, 8, 8, 12, 12, 4, 4, 8, 8, 8, 8, 4, 4, 8, 8, 8, 8, 4, 4, 8, 8, 4, 4, 12, 12]
    fin, down, grad_voxels = pl.pallas_call(
        main_kernel,
        out_shape=(
            pltpu.VMEM((2, ROWS, LANES), BF16),
            pltpu.VMEM((64, C), BF16),
            pltpu.VMEM((512, C), BF16),
        ),
        in_specs=[anywhere] * 6,
        out_specs=(vmem, vmem, vmem),
        scratch_shapes=[pltpu.VMEM(shape, dtype) for shape, dtype in scratch]
        + [pltpu.SemaphoreType.DMA((n,)) for n in semaphores],
        compiler_params=pltpu.CompilerParams(
            collective_id=0, has_side_effects=True, vmem_limit_bytes=56 * 1024 * 1024
        ),
    )(
        voxels.reshape(512, C),
        occupancy.reshape(64, DEEP),
        conv_weight,
        conv_bias.reshape(1, C),
        down_weight,
        down_cotangent.reshape(64, C),
    )
    cells = voxels.shape[0] * lax.axis_size("gx") * voxels.shape[1] * lax.axis_size("gy") * DEEP
    factor = 1.0 / math.sqrt(cells)
    down, grad_voxels, grad_conv, grad_bias, grad_down = pl.pallas_call(
        lambda *refs: finish_kernel(factor, *refs),
        out_shape=(
            jax.ShapeDtypeStruct((64, C), BF16),
            jax.ShapeDtypeStruct((512, C), BF16),
            jax.ShapeDtypeStruct((TAPS, C, C), F32),
            jax.ShapeDtypeStruct((1, C), F32),
            jax.ShapeDtypeStruct((TAPS, C, C), F32),
        ),
        in_specs=[vmem] * 3,
        out_specs=(anywhere,) * 5,
        scratch_shapes=[
            pltpu.VMEM((TAPS, C, C), F32),
            pltpu.VMEM((1, C), F32),
            pltpu.VMEM((TAPS, C, C), F32),
            pltpu.SemaphoreType.DMA((17,)),
        ],
        compiler_params=pltpu.CompilerParams(vmem_limit_bytes=32 * 1024 * 1024),
    )(fin, down, grad_voxels)
    return (
        down.reshape(down_cotangent.shape),
        grad_voxels.reshape(voxels.shape),
        grad_conv,
        grad_bias.reshape(C),
        grad_down,
    )


def solution(mesh):
    tile = P("gx", "gy", None, None)
    return jax.shard_map(
        on_device,
        mesh=mesh,
        in_specs=(tile, P("gx", "gy", None), P(), P(), P(), tile),
        out_specs=(tile, tile, P(), P(), P()),
        check_vma=False,
    )
```

```python
import math

import jax
import jax.numpy as jnp
from jax import lax
from jax.experimental import pallas as pl
from jax.experimental.pallas import tpu as pltpu
from jax.sharding import PartitionSpec as P

F32 = jnp.float32
BF16 = jnp.bfloat16
MESH = pl.DeviceIdType.MESH

C = 96
LANES = 128
TAPS = 27
TILE = 8
HALF = 4
DEEP = 8
K_ALL = TAPS * LANES
ROWS = 2048
PARTS = ((0, 32), (1024, 32))
NX, NY, NZ = 4, 8, 8
TAP_OFFSETS = [(a, b, e) for a in (-1, 0, 1) for b in (-1, 0, 1) for e in (-1, 0, 1)]

SIDES = [(-1, 0), (1, 0), (0, -1), (0, 1), (-1, -1), (-1, 1), (1, -1), (1, 1)]
SIDE_ROWS = [160 if 0 in side else 48 for side in SIDES]
SIDE_AT = [sum(SIDE_ROWS[:i]) for i in range(8)]
HALO_ROWS = sum(SIDE_ROWS)

PIECES = [
    (0, 1, 8, 1, 8),
    (512, 0, 1, 0, 10),
    (592, 9, 1, 0, 10),
    (672, 1, 8, 0, 1),
    (736, 1, 8, 9, 1),
]


def edge(step, length, width):
    return {-1: (0, width), 0: (0, length), 1: (length - width, width)}[step]


def landing(step, length, width):
    return {-1: (0, width), 0: (width, length), 1: (width + length, width)}[step]


def dot(left, right):
    return lax.dot_general(left, right, (((1,), (0,)), ((), ())), preferred_element_type=F32)


def dot_nt(left, right):
    return lax.dot_general(left, right, (((1,), (1,)), ((), ())), preferred_element_type=F32)


def iota(shape, dim):
    return lax.broadcasted_iota(jnp.int32, shape, dim)


def z_shifts(value):
    columns = value.shape[0]
    level = iota((columns, DEEP, LANES), 1)
    below = jnp.where(level == 0, 0.0, pltpu.roll(value, 1, 1))
    above = jnp.where(level == DEEP - 1, 0.0, pltpu.roll(value, DEEP - 1, 1))
    return below, value, above


def store_shifts(ref, value, at_x, size_x, at_y, size_y):
    for k, shifted in enumerate(z_shifts(value.reshape(size_x * size_y, DEEP, LANES))):
        ref[k, at_x : at_x + size_x, at_y : at_y + size_y] = shifted.reshape(
            size_x, size_y, DEEP, LANES
        )


def dense_tiles(acc, extra):
    lane = iota((C, LANES), 1)
    tap = lambda t: acc[:, t * LANES : (t + 1) * LANES]
    tiles = []
    for group in range(7):
        first = 4 * group
        one = pltpu.roll(tap(first + 1), 96, 1)
        two = pltpu.roll(tap(first + 2), 64, 1)
        tiles.append(jnp.where(lane < 96, tap(first), one))
        tiles.append(jnp.where(lane < 64, one, two))
        if group < 6:
            three = pltpu.roll(tap(first + 3), 32, 1)
        else:
            three = jnp.where(lane == 32, pltpu.roll(extra, 64, 1), 0.0)
        tiles.append(jnp.where(lane < 32, two, three))
    return tiles


def main_kernel(
    vox_hbm, occ_hbm, cw_hbm, bias_hbm, dw_hbm, cot_hbm,
    fin_ref, down_ref, gv_ref,
    vox_ref, occ_ref, cw_ref, bias_ref, dw_ref, cot_ref, bias_row,
    hs, hr, a3, c3, gs10, s3, g3, pre, p1, p2, ps, wf, wb, df, db, cl,
    part, rc, xa, xa_in, nb, nb_in, na, na_in, xb, xb_in, far_in,
    in_sem, h_send, h_recv, c_send, c_recv, xa_send, xa_recv, nb_send, nb_recv,
    na_send, na_recv, xb_send, xb_recv, far_send, far_recv,
    gna_send, gna_recv, gxb_send, gxb_recv, gnb_send, gnb_recv, gxa_send, gxa_recv,
    gc_send, gc_recv,
):
    gx = lax.axis_index("gx")
    gy = lax.axis_index("gy")
    n_gx = lax.axis_size("gx")
    n_gy = lax.axis_size("gy")
    px, pz = gx // NZ, gx % NZ
    py, core = gy // 2, gy % 2
    sibling = (gx, gy + 1 - 2 * core)
    side_peer = [((gx + sx + n_gx) % n_gx, (gy + sy + n_gy) % n_gy) for sx, sy in SIDES]
    x_peer = [(((px + k) % NX) * NZ + pz, gy) for k in range(NX)]
    y_peer = [(gx, ((py + k) % NY) * 2 + core) for k in range(NY)]
    z_peer = [(px * NZ + (pz + k) % NZ, gy) for k in range(NZ)]

    def chosen(first, second):
        return tuple(i + core * (j - i) for i, j in zip(first, second))

    near = [chosen(y_peer[k], z_peer[k]) for k in range(8)]
    far = [chosen(z_peer[k], y_peer[k]) for k in range(8)]
    i_near = py + core * (pz - py)
    i_far = pz + core * (py - pz)

    barrier = pltpu.get_barrier_semaphore()
    greeted = side_peer + [sibling] + x_peer[1:] + y_peer[1:] + z_peer[1:]
    for peer in greeted:
        pl.semaphore_signal(barrier, inc=1, device_id=peer, device_id_type=MESH)

    loads = [
        pltpu.make_async_copy(src, dst, in_sem.at[i])
        for i, (src, dst) in enumerate(
            (
                (occ_hbm, occ_ref),
                (vox_hbm, vox_ref),
                (cot_hbm, cot_ref),
                (cw_hbm, cw_ref),
                (dw_hbm, dw_ref),
                (bias_hbm, bias_ref),
            )
        )
    ]
    for load in loads:
        load.start()

    def remote(src, dst, send, recv, peer):
        return pltpu.make_async_remote_copy(
            src_ref=src, dst_ref=dst, send_sem=send, recv_sem=recv, device_id=peer,
            device_id_type=MESH,
        )

    def await_bytes(ref, semaphore):
        pltpu.make_async_copy(ref, ref, semaphore).wait()

    for load in loads[:3]:
        load.wait()

    spread = (iota((512, 64), 0) // DEEP == iota((512, 64), 1)).astype(BF16)
    by_column = dot(spread, occ_ref[...].astype(F32).astype(BF16))
    own_level = iota((512, DEEP), 0) % DEEP == iota((512, DEEP), 1)
    picked = jnp.where(own_level, by_column, 0.0).astype(BF16)
    live = dot(picked, jnp.ones((DEEP, LANES), BF16))
    widen = (iota((C, LANES), 0) == iota((C, LANES), 1)).astype(BF16)
    lane512 = iota((512, LANES), 1)
    masked = jnp.where(lane512 == C, live, dot(vox_ref[...], widen) * live)
    masked = masked.reshape(TILE, TILE, DEEP, LANES)
    pairs = live.reshape(HALF, 2, HALF, 2, DEEP, LANES)
    most = jnp.maximum(
        jnp.maximum(pairs[:, 0, :, 0], pairs[:, 0, :, 1]),
        jnp.maximum(pairs[:, 1, :, 0], pairs[:, 1, :, 1]),
    ).reshape(HALF * HALF, DEEP, LANES)
    coarse_live = jnp.maximum(most, pltpu.roll(most, DEEP - 1, 1)).reshape(128, LANES)
    cl[...] = coarse_live
    upward = (iota((128, 64), 0) == 2 * iota((128, 64), 1)).astype(BF16)
    cot = (dot(upward, dot(cot_ref[...], widen).astype(BF16)) * coarse_live).reshape(
        HALF, HALF, DEEP, LANES
    )

    for i, (sx, sy) in enumerate(SIDES):
        x0, wx = edge(sx, TILE, 2)
        y0, wy = edge(sy, TILE, 2)
        rows = wx * wy * DEEP
        at = SIDE_AT[i]
        hs[at : at + rows, :] = (
            masked[x0 : x0 + wx, y0 : y0 + wy].reshape(rows, LANES).astype(BF16)
        )
        x0, wx = edge(sx, HALF, 1)
        y0, wy = edge(sy, HALF, 1)
        more = wx * wy * DEEP
        block = cot[x0 : x0 + wx, y0 : y0 + wy].reshape(more, LANES)
        if more < 16:
            block = jnp.concatenate([block, jnp.zeros((16 - more, LANES), F32)], 0)
        hs[at + rows : at + SIDE_ROWS[i], :] = block.astype(BF16)

    pl.semaphore_wait(barrier, len(greeted))
    for i, (sx, sy) in enumerate(SIDES):
        there = SIDES.index((-sx, -sy))
        mine = pl.ds(SIDE_AT[i], SIDE_ROWS[i])
        theirs = pl.ds(SIDE_AT[there], SIDE_ROWS[i])
        copy = remote(hs.at[mine], hr.at[theirs], h_send.at[0], h_recv.at[0], side_peer[i])
        copy.start()

    store_shifts(a3, masked, 2, TILE, 2, TILE)
    store_shifts(c3, cot, 1, HALF, 1, HALF)
    for ref in (wf, wb, df, db):
        ref[...] = jnp.zeros(ref.shape, BF16)
    bias_row[...] = jnp.zeros((1, LANES), F32)
    for load in loads[3:]:
        load.wait()
    bias_row[:, 0:C] = bias_ref[...]
    for t in range(TAPS):
        for source, plain, turned in ((cw_ref, wf, wb), (dw_ref, df, db)):
            block = source[t]
            plain[t * LANES : t * LANES + C, 0:C] = block
            turned[0:C, t * LANES : t * LANES + C] = block
    for w in (0, 1):
        part[w, 2016:2048, :] = jnp.zeros((32, LANES), BF16)

    await_bytes(hs, h_send.at[0])
    await_bytes(hr, h_recv.at[0])
    for i, (sx, sy) in enumerate(SIDES):
        inside = 1.0
        for step, at, size in ((sx, gx, n_gx), (sy, gy, n_gy)):
            if step:
                inside = inside * jnp.where(at == (0 if step < 0 else size - 1), 0.0, 1.0)
        at = SIDE_AT[i]
        x0, wx = landing(sx, TILE, 2)
        y0, wy = landing(sy, TILE, 2)
        rows = wx * wy * DEEP
        store_shifts(a3, hr[at : at + rows, :].astype(F32) * inside, x0, wx, y0, wy)
        x0, wx = landing(sx, HALF, 1)
        y0, wy = landing(sy, HALF, 1)
        more = wx * wy * DEEP
        block = hr[at + rows : at + SIDE_ROWS[i], :].astype(F32)[:more] * inside
        store_shifts(c3, block, x0, wx, y0, wy)

    for t, (a, b, e) in enumerate(TAP_OFFSETS):
        lanes = slice(t * LANES, (t + 1) * LANES)
        for row, x0, wx, y0, wy in PIECES:
            x1, y1 = x0 + 1 + a, y0 + 1 + b
            rows = wx * wy * DEEP
            window = a3[e + 1, x1 : x1 + wx, y1 : y1 + wy]
            p1[row : row + rows, lanes] = window.reshape(rows, LANES).astype(BF16)
    pre[...] = dot(p1[...], wf[...]) + bias_row[...]

    for parity_x in (0, 1):
        for parity_y in (0, 1):
            total = None
            for a in ((-1, 1) if parity_x else (0,)):
                for b in ((-1, 1) if parity_y else (0,)):
                    x0 = 0 if a == 1 else 1
                    y0 = 0 if b == 1 else 1
                    windows = [
                        c3[1 - e, x0 : x0 + 5, y0 : y0 + 5].reshape(200, LANES).astype(BF16)
                        for e in (-1, 0, 1)
                    ]
                    t = 9 * (a + 1) + 3 * (b + 1)
                    term = dot_nt(
                        jnp.concatenate(windows, 1), db[:, t * LANES : (t + 3) * LANES]
                    )
                    total = term if total is None else total + term
            gs10[:, 1 - parity_x, :, 1 - parity_y] = total.reshape(5, 5, DEEP, LANES)

    pick_live = (iota((LANES, LANES), 0) == C).astype(BF16)
    ten = gs10.reshape(10, 10, DEEP, LANES)
    for row, x0, wx, y0, wy in PIECES:
        rows = wx * wy * DEEP
        value = pre[row : row + rows, :]
        feature = p1[row : row + rows, 13 * LANES : 14 * LANES]
        alive = dot(feature, pick_live)
        gate = 1.0 / (1.0 + jnp.exp(-value))
        summed = (feature.astype(F32) + alive * (value * gate)).astype(BF16).astype(F32)
        grad_sum = ten[x0 : x0 + wx, y0 : y0 + wy].reshape(rows, LANES)
        grad_pre = grad_sum * alive * gate * (1.0 + value * (1.0 - gate))
        store_shifts(s3, summed, x0, wx, y0, wy)
        store_shifts(g3, grad_pre.astype(BF16).astype(F32), x0, wx, y0, wy)

    six = s3.reshape(3, 5, 2, 5, 2, DEEP, LANES)
    for t, (a, b, e) in enumerate(TAP_OFFSETS):
        i0, si = (a + 1) // 2, (a + 1) % 2
        j0, sj = (b + 1) // 2, (b + 1) % 2
        window = six[e + 1, i0 : i0 + 4, si, j0 : j0 + 4, sj]
        ps[:, t * LANES : (t + 1) * LANES] = window.reshape(128, LANES).astype(BF16)
    far_first = (4, 3, 5, 2, 6, 1, 7)
    near_first = (1, 7, 2, 6, 3, 5, 4)

    def rows(which, place):
        start, size = PARTS[which]
        return pl.ds(pl.multiple_of(start + place * 4 * size, 64), 4 * size)

    def block_rows(which, place, x):
        start, size = PARTS[which]
        return pl.ds(pl.multiple_of(start + place * 4 * size + x * size, 16), size)

    order = [(which, j) for j in far_first + (0,) for which in (0, 1)]
    core_copies = []
    for which, j in order:
        there = rows(which, (i_far + j) % 8)
        core_copies.append(
            remote(part.at[1 - core, there], rc.at[there], c_send.at[0], c_recv.at[j], sibling)
        )

    def down_sums():
        cot_turned = c3[1, 1:5, 1:5].reshape(128, LANES).T[0:C].astype(BF16)
        acc = dot(cot_turned, ps[...])
        for j, tile in enumerate(dense_tiles(acc, jnp.zeros((C, LANES), F32))):
            part[1, j * C : (j + 1) * C, :] = tile.astype(BF16)

    def conv_sums():
        pre_turned = g3[1, 1:9, 1:9].reshape(512, LANES).T[0:C].astype(BF16)
        acc = dot(pre_turned, p1[0:512, :])
        for j, tile in enumerate(dense_tiles(acc, acc[:, 13 * LANES : 14 * LANES])):
            part[0, j * C : (j + 1) * C, :] = tile.astype(BF16)

    @pl.when(core == 0)
    def _():
        down_sums()
        for copy in core_copies:
            copy.start()
        conv_sums()

    @pl.when(core == 1)
    def _():
        conv_sums()
        for copy in core_copies:
            copy.start()
        down_sums()

    for which, j in order:
        if which == 0:
            await_bytes(rc.at[0:256], c_recv.at[j])
        here = rows(which, (i_near + j) % 8)
        both = (part[core, here].astype(F32) + rc[here].astype(F32)).astype(BF16)
        if which == 0:
            xa[j] = both.reshape(4, 32, LANES)
            for k in (2, 1, 3):
                remote(
                    xa.at[j, (px + k) % NX], xa_in.at[j, k], xa_send.at[0], xa_recv.at[j], x_peer[k]
                ).start()
        else:
            nb[j] = both
            if j:
                remote(nb.at[j], nb_in.at[j], nb_send.at[0], nb_recv.at[0], near[j]).start()

    downward = (iota((64, 128), 1) == 2 * iota((64, 128), 0)).astype(BF16)
    coarse = (dot(ps[...], df[...]) * cl[...]).astype(BF16)
    down_ref[...] = dot(downward, coarse).astype(BF16)[:, 0:C]

    for t, (a, b, e) in enumerate(TAP_OFFSETS):
        window = g3[1 - e, 1 - a : 9 - a, 1 - b : 9 - b]
        p2[:, t * LANES : (t + 1) * LANES] = window.reshape(512, LANES).astype(BF16)
    grad_in = ten[1:9, 1:9].reshape(512, LANES) + dot_nt(p2[...], wb[...])
    alive = dot(p1[0:512, 13 * LANES : 14 * LANES], pick_live)
    gv_ref[...] = (grad_in * alive).astype(BF16)[:, 0:C]

    for j in far_first + (0,):
        await_bytes(xa_in.at[j, 1:4], xa_recv.at[j])
        total = xa[j, px].astype(F32)
        for k in (1, 3, 2):
            total = total + xa_in[j, k].astype(F32)
        na[j] = total.astype(BF16)
        if j:
            remote(na.at[j], na_in.at[j], na_send.at[0], na_recv.at[0], near[j]).start()
    await_bytes(nb_in.at[1:8], nb_recv.at[0])
    total = nb[0].astype(F32)
    for k in near_first:
        total = total + nb_in[k].astype(F32)
    xb[...] = total.reshape(4, 32, LANES).astype(BF16)
    for k in (2, 1, 3):
        remote(xb.at[(px + k) % NX], xb_in.at[k], xb_send.at[0], xb_recv.at[0], x_peer[k]).start()

    await_bytes(na_in.at[1:8], na_recv.at[0])
    total = na[0].astype(F32)
    for k in near_first:
        total = total + na_in[k].astype(F32)
    far_in[i_far, 0:32] = total.astype(BF16)
    await_bytes(xb_in.at[1:4], xb_recv.at[0])
    total = xb[px].astype(F32)
    for k in (1, 3, 2):
        total = total + xb_in[k].astype(F32)
    far_in[i_far, 32:64] = total.astype(BF16)
    for k in far_first:
        block = far_in.at[i_far]
        remote(block, block, far_send.at[0], far_recv.at[0], far[k]).start()
    await_bytes(far_in.at[0:7], far_recv.at[0])
    total = far_in[0].astype(F32)
    for k in range(1, 8):
        total = total + far_in[k].astype(F32)
    total = total.astype(BF16)

    fin_ref[core, block_rows(0, i_near, px)] = total[0:32]
    fin_ref[core, block_rows(1, i_near, px)] = total[32:64]

    block = fin_ref.at[core, block_rows(0, i_near, px)]
    for k in far_first:
        remote(block, block, gna_send.at[0], gna_recv.at[k], near[k]).start()
    block = fin_ref.at[core, block_rows(1, i_near, px)]
    for k in (2, 1, 3):
        remote(block, block, gxb_send.at[0], gxb_recv.at[0], x_peer[k]).start()

    def across(j):
        if j:
            await_bytes(na_in.at[j], gna_recv.at[j])
        block = fin_ref.at[core, block_rows(0, (i_near - j + 8) % 8, px)]
        for k in (2, 1, 3):
            remote(block, block, gxa_send.at[0], gxa_recv.at[j], x_peer[k]).start()

    def hand_over(which, j):
        block = fin_ref.at[core, rows(which, (i_near - j + 8) % 8)]
        remote(block, block, gc_send.at[0], gc_recv.at[0], sibling).start()

    for j in (0, 1, 7):
        across(j)
    await_bytes(xb_in.at[1:4], gxb_recv.at[0])
    block = fin_ref.at[core, rows(1, i_near)]
    for k in far_first:
        remote(block, block, gnb_send.at[0], gnb_recv.at[k], near[k]).start()
    for j in (2, 6, 3, 5, 4):
        across(j)
    for j in (0,) + near_first:
        await_bytes(xa_in.at[j, 1:4], gxa_recv.at[j])
        hand_over(0, j)
        if j:
            await_bytes(nb_in.at[j], gnb_recv.at[j])
        hand_over(1, j)
    for ref, sends in (
        (rc, c_send),
        (xa_in.at[:, 1:4], xa_send),
        (nb_in.at[1:8], nb_send),
        (na_in.at[1:8], na_send),
        (xb_in.at[1:4], xb_send),
        (far_in.at[0:7], far_send),
        (na_in.at[1:8], gna_send),
        (xb_in.at[1:4], gxb_send),
        (xa_in.at[:, 1:4], gxa_send),
        (nb_in.at[1:8], gnb_send),
        (rc, gc_send),
        (rc, gc_recv),
    ):
        await_bytes(ref, sends.at[0])


def finish_kernel(
    factor, fin_ref, down_in, gv_in, down_ref, gv_ref, gc_ref, gb_ref, gd_ref,
    gc, gb, gd, sem,
):
    copies = []

    def send_out(src, dst):
        copies.append(pltpu.make_async_copy(src, dst, sem.at[len(copies)]))
        copies[-1].start()

    send_out(down_in, down_ref)
    send_out(gv_in, gv_ref)
    lane = iota((C, LANES), 1)
    for w, held, out in ((1, gd, gd_ref), (0, gc, gc_ref)):
        for group in range(7):
            first, second, third = (
                fin_ref[w, (3 * group + i) * C : (3 * group + i + 1) * C, :].astype(F32) * factor
                for i in range(3)
            )
            taps = [
                first,
                pltpu.roll(jnp.where(lane >= 96, first, second), 32, 1),
                pltpu.roll(jnp.where(lane >= 64, second, third), 64, 1),
                pltpu.roll(third, 96, 1),
            ]
            count = 4 if group < 6 else 3
            for i in range(count):
                held[4 * group + i] = taps[i].T[0:C]
            block = pl.ds(4 * group, count)
            send_out(held.at[block], out.at[block])
        if w == 0:
            gb[...] = third.T[32:33]
            send_out(gb, gb_ref)
    for copy in copies:
        copy.wait()


def on_device(voxels, occupancy, conv_weight, conv_bias, down_weight, down_cotangent):
    vmem = pl.BlockSpec(memory_space=pltpu.VMEM)
    anywhere = pl.BlockSpec(memory_space=pl.ANY)
    scratch = [
        ((512, C), BF16),
        ((64, DEEP), jnp.int32),
        ((TAPS, C, C), BF16),
        ((1, C), F32),
        ((TAPS, C, C), BF16),
        ((64, C), BF16),
        ((1, LANES), F32),
        ((HALO_ROWS, LANES), BF16),
        ((HALO_ROWS, LANES), BF16),
        ((3, 12, 12, DEEP, LANES), F32),
        ((3, 6, 6, DEEP, LANES), F32),
        ((5, 2, 5, 2, DEEP, LANES), F32),
        ((3, 10, 10, DEEP, LANES), F32),
        ((3, 10, 10, DEEP, LANES), F32),
        ((800, LANES), F32),
        ((800, K_ALL), BF16),
        ((512, K_ALL), BF16),
        ((128, K_ALL), BF16),
        ((K_ALL, LANES), BF16),
        ((LANES, K_ALL), BF16),
        ((K_ALL, LANES), BF16),
        ((LANES, K_ALL), BF16),
        ((128, LANES), F32),
        ((2, ROWS, LANES), BF16),
        ((ROWS, LANES), BF16),
        ((8, 4, 32, LANES), BF16),
        ((8, 4, 32, LANES), BF16),
        ((8, 128, LANES), BF16),
        ((8, 128, LANES), BF16),
        ((8, 32, LANES), BF16),
        ((8, 32, LANES), BF16),
        ((4, 32, LANES), BF16),
        ((4, 32, LANES), BF16),
        ((8, 64, LANES), BF16),
    ]
    semaphores = [6, 1, 1, 1, 8, 1, 8, 1, 1, 1, 1, 1, 1, 1, 1, 1, 8, 1, 1, 1, 8, 1, 8, 1, 1]
    fin, down, grad_voxels = pl.pallas_call(
        main_kernel,
        out_shape=(
            pltpu.VMEM((2, ROWS, LANES), BF16),
            pltpu.VMEM((64, C), BF16),
            pltpu.VMEM((512, C), BF16),
        ),
        in_specs=[anywhere] * 6,
        out_specs=(vmem, vmem, vmem),
        scratch_shapes=[pltpu.VMEM(shape, dtype) for shape, dtype in scratch]
        + [pltpu.SemaphoreType.DMA((n,)) for n in semaphores],
        compiler_params=pltpu.CompilerParams(
            collective_id=0, has_side_effects=True, vmem_limit_bytes=56 * 1024 * 1024
        ),
    )(
        voxels.reshape(512, C),
        occupancy.reshape(64, DEEP),
        conv_weight,
        conv_bias.reshape(1, C),
        down_weight,
        down_cotangent.reshape(64, C),
    )
    cells = voxels.shape[0] * lax.axis_size("gx") * voxels.shape[1] * lax.axis_size("gy") * DEEP
    factor = 1.0 / math.sqrt(cells)
    down, grad_voxels, grad_conv, grad_bias, grad_down = pl.pallas_call(
        lambda *refs: finish_kernel(factor, *refs),
        out_shape=(
            jax.ShapeDtypeStruct((64, C), BF16),
            jax.ShapeDtypeStruct((512, C), BF16),
            jax.ShapeDtypeStruct((TAPS, C, C), F32),
            jax.ShapeDtypeStruct((1, C), F32),
            jax.ShapeDtypeStruct((TAPS, C, C), F32),
        ),
        in_specs=[vmem] * 3,
        out_specs=(anywhere,) * 5,
        scratch_shapes=[
            pltpu.VMEM((TAPS, C, C), F32),
            pltpu.VMEM((1, C), F32),
            pltpu.VMEM((TAPS, C, C), F32),
            pltpu.SemaphoreType.DMA((17,)),
        ],
        compiler_params=pltpu.CompilerParams(vmem_limit_bytes=32 * 1024 * 1024),
    )(fin, down, grad_voxels)
    return (
        down.reshape(down_cotangent.shape),
        grad_voxels.reshape(voxels.shape),
        grad_conv,
        grad_bias.reshape(C),
        grad_down,
    )


def solution(mesh):
    tile = P("gx", "gy", None, None)
    return jax.shard_map(
        on_device,
        mesh=mesh,
        in_specs=(tile, P("gx", "gy", None), P(), P(), P(), tile),
        out_specs=(tile, tile, P(), P(), P()),
        check_vma=False,
    )
```

```python
import math

import jax
import jax.numpy as jnp
from jax import lax
from jax.experimental import pallas as pl
from jax.experimental.pallas import tpu as pltpu
from jax.sharding import PartitionSpec as P

F32 = jnp.float32
BF16 = jnp.bfloat16
MESH = pl.DeviceIdType.MESH

C = 96
LANES = 128
TAPS = 27
TILE = 8
HALF = 4
DEEP = 8
K_ALL = TAPS * LANES
ROWS = 2048
PARTS = ((0, 32), (1024, 32))
NX, NY, NZ = 4, 8, 8
TAP_OFFSETS = [(a, b, e) for a in (-1, 0, 1) for b in (-1, 0, 1) for e in (-1, 0, 1)]

SIDES = [(-1, 0), (1, 0), (0, -1), (0, 1), (-1, -1), (-1, 1), (1, -1), (1, 1)]
SIDE_ROWS = [160 if 0 in side else 48 for side in SIDES]
SIDE_AT = [sum(SIDE_ROWS[:i]) for i in range(8)]
HALO_ROWS = sum(SIDE_ROWS)

PIECES = [
    (0, 1, 8, 1, 8),
    (512, 0, 1, 0, 10),
    (592, 9, 1, 0, 10),
    (672, 1, 8, 0, 1),
    (736, 1, 8, 9, 1),
]


def edge(step, length, width):
    return {-1: (0, width), 0: (0, length), 1: (length - width, width)}[step]


def landing(step, length, width):
    return {-1: (0, width), 0: (width, length), 1: (width + length, width)}[step]


def dot(left, right):
    return lax.dot_general(left, right, (((1,), (0,)), ((), ())), preferred_element_type=F32)


def dot_nt(left, right):
    return lax.dot_general(left, right, (((1,), (1,)), ((), ())), preferred_element_type=F32)


def iota(shape, dim):
    return lax.broadcasted_iota(jnp.int32, shape, dim)


def z_shifts(value):
    columns = value.shape[0]
    level = iota((columns, DEEP, LANES), 1)
    below = jnp.where(level == 0, 0.0, pltpu.roll(value, 1, 1))
    above = jnp.where(level == DEEP - 1, 0.0, pltpu.roll(value, DEEP - 1, 1))
    return below, value, above


def store_shifts(ref, value, at_x, size_x, at_y, size_y):
    for k, shifted in enumerate(z_shifts(value.reshape(size_x * size_y, DEEP, LANES))):
        ref[k, at_x : at_x + size_x, at_y : at_y + size_y] = shifted.reshape(
            size_x, size_y, DEEP, LANES
        )


def dense_tiles(acc, extra):
    lane = iota((C, LANES), 1)
    tap = lambda t: acc[:, t * LANES : (t + 1) * LANES]
    tiles = []
    for group in range(7):
        first = 4 * group
        one = pltpu.roll(tap(first + 1), 96, 1)
        two = pltpu.roll(tap(first + 2), 64, 1)
        tiles.append(jnp.where(lane < 96, tap(first), one))
        tiles.append(jnp.where(lane < 64, one, two))
        if group < 6:
            three = pltpu.roll(tap(first + 3), 32, 1)
        else:
            three = jnp.where(lane == 32, pltpu.roll(extra, 64, 1), 0.0)
        tiles.append(jnp.where(lane < 32, two, three))
    return tiles


def main_kernel(
    vox_hbm, occ_hbm, cw_hbm, bias_hbm, dw_hbm, cot_hbm,
    fin_ref, down_ref, gv_ref,
    vox_ref, occ_ref, cw_ref, bias_ref, dw_ref, cot_ref, bias_row,
    hs, hr, a3, c3, gs10, s3, g3, pre, p1, p2, ps, wf, wb, df, db, cl,
    part, rc, xa, xa_in, nb, nb_in, na, na_in, xb, xb_in, far_in,
    in_sem, h_send, h_recv, c_send, c_recv, xa_send, xa_recv, nb_send, nb_recv,
    na_send, na_recv, xb_send, xb_recv, far_send, far_recv,
    gna_send, gna_recv, gxb_send, gxb_recv, gnb_send, gnb_recv, gxa_send, gxa_recv,
    gc_send, gc_recv,
):
    gx = lax.axis_index("gx")
    gy = lax.axis_index("gy")
    n_gx = lax.axis_size("gx")
    n_gy = lax.axis_size("gy")
    px, pz = gx // NZ, gx % NZ
    py, core = gy // 2, gy % 2
    sibling = (gx, gy + 1 - 2 * core)
    side_peer = [((gx + sx + n_gx) % n_gx, (gy + sy + n_gy) % n_gy) for sx, sy in SIDES]
    x_peer = [(((px + k) % NX) * NZ + pz, gy) for k in range(NX)]
    y_peer = [(gx, ((py + k) % NY) * 2 + core) for k in range(NY)]
    z_peer = [(px * NZ + (pz + k) % NZ, gy) for k in range(NZ)]

    def chosen(first, second):
        return tuple(i + core * (j - i) for i, j in zip(first, second))

    near = [chosen(y_peer[k], z_peer[k]) for k in range(8)]
    far = [chosen(z_peer[k], y_peer[k]) for k in range(8)]
    i_near = py + core * (pz - py)
    i_far = pz + core * (py - pz)

    barrier = pltpu.get_barrier_semaphore()
    greeted = [peer for k in (4, 3, 5, 2, 6) for peer in (y_peer[k], z_peer[k])]
    greeted += [x_peer[2]] + side_peer[4:] + [x_peer[1], x_peer[3]]
    greeted += [y_peer[1], z_peer[1], y_peer[7], z_peer[7]] + side_peer[:4]
    for peer in greeted:
        pl.semaphore_signal(barrier, inc=1, device_id=peer, device_id_type=MESH)

    loads = [
        pltpu.make_async_copy(src, dst, in_sem.at[i])
        for i, (src, dst) in enumerate(
            (
                (occ_hbm, occ_ref),
                (vox_hbm, vox_ref),
                (cot_hbm, cot_ref),
                (cw_hbm, cw_ref),
                (dw_hbm, dw_ref),
                (bias_hbm, bias_ref),
            )
        )
    ]
    for load in loads:
        load.start()

    def remote(src, dst, send, recv, peer):
        return pltpu.make_async_remote_copy(
            src_ref=src, dst_ref=dst, send_sem=send, recv_sem=recv, device_id=peer,
            device_id_type=MESH,
        )

    def await_bytes(ref, semaphore):
        pltpu.make_async_copy(ref, ref, semaphore).wait()

    for load in loads[:3]:
        load.wait()

    spread = (iota((512, 64), 0) // DEEP == iota((512, 64), 1)).astype(BF16)
    by_column = dot(spread, occ_ref[...].astype(F32).astype(BF16))
    own_level = iota((512, DEEP), 0) % DEEP == iota((512, DEEP), 1)
    picked = jnp.where(own_level, by_column, 0.0).astype(BF16)
    live = dot(picked, jnp.ones((DEEP, LANES), BF16))
    widen = (iota((C, LANES), 0) == iota((C, LANES), 1)).astype(BF16)
    lane512 = iota((512, LANES), 1)
    masked = jnp.where(lane512 == C, live, dot(vox_ref[...], widen) * live)
    masked = masked.reshape(TILE, TILE, DEEP, LANES)
    pairs = live.reshape(HALF, 2, HALF, 2, DEEP, LANES)
    most = jnp.maximum(
        jnp.maximum(pairs[:, 0, :, 0], pairs[:, 0, :, 1]),
        jnp.maximum(pairs[:, 1, :, 0], pairs[:, 1, :, 1]),
    ).reshape(HALF * HALF, DEEP, LANES)
    coarse_live = jnp.maximum(most, pltpu.roll(most, DEEP - 1, 1)).reshape(128, LANES)
    cl[...] = coarse_live
    upward = (iota((128, 64), 0) == 2 * iota((128, 64), 1)).astype(BF16)
    cot = (dot(upward, dot(cot_ref[...], widen).astype(BF16)) * coarse_live).reshape(
        HALF, HALF, DEEP, LANES
    )

    for i, (sx, sy) in enumerate(SIDES):
        x0, wx = edge(sx, TILE, 2)
        y0, wy = edge(sy, TILE, 2)
        rows = wx * wy * DEEP
        at = SIDE_AT[i]
        hs[at : at + rows, :] = (
            masked[x0 : x0 + wx, y0 : y0 + wy].reshape(rows, LANES).astype(BF16)
        )
        x0, wx = edge(sx, HALF, 1)
        y0, wy = edge(sy, HALF, 1)
        more = wx * wy * DEEP
        block = cot[x0 : x0 + wx, y0 : y0 + wy].reshape(more, LANES)
        if more < 16:
            block = jnp.concatenate([block, jnp.zeros((16 - more, LANES), F32)], 0)
        hs[at + rows : at + SIDE_ROWS[i], :] = block.astype(BF16)

    pl.semaphore_wait(barrier, len(greeted))
    for i in (4, 5, 6, 7, 0, 1, 2, 3):
        sx, sy = SIDES[i]
        there = SIDES.index((-sx, -sy))
        mine = pl.ds(SIDE_AT[i], SIDE_ROWS[i])
        theirs = pl.ds(SIDE_AT[there], SIDE_ROWS[i])
        copy = remote(hs.at[mine], hr.at[theirs], h_send.at[0], h_recv.at[0], side_peer[i])
        copy.start()

    store_shifts(a3, masked, 2, TILE, 2, TILE)
    store_shifts(c3, cot, 1, HALF, 1, HALF)
    for ref in (wf, wb, df, db):
        ref[...] = jnp.zeros(ref.shape, BF16)
    bias_row[...] = jnp.zeros((1, LANES), F32)
    for load in loads[3:]:
        load.wait()
    bias_row[:, 0:C] = bias_ref[...]
    for t in range(TAPS):
        for source, plain, turned in ((cw_ref, wf, wb), (dw_ref, df, db)):
            block = source[t]
            plain[t * LANES : t * LANES + C, 0:C] = block
            turned[0:C, t * LANES : t * LANES + C] = block
    for w in (0, 1):
        part[w, 2016:2048, :] = jnp.zeros((32, LANES), BF16)

    await_bytes(hs, h_send.at[0])
    await_bytes(hr, h_recv.at[0])
    for i, (sx, sy) in enumerate(SIDES):
        inside = 1.0
        for step, at, size in ((sx, gx, n_gx), (sy, gy, n_gy)):
            if step:
                inside = inside * jnp.where(at == (0 if step < 0 else size - 1), 0.0, 1.0)
        at = SIDE_AT[i]
        x0, wx = landing(sx, TILE, 2)
        y0, wy = landing(sy, TILE, 2)
        rows = wx * wy * DEEP
        store_shifts(a3, hr[at : at + rows, :].astype(F32) * inside, x0, wx, y0, wy)
        x0, wx = landing(sx, HALF, 1)
        y0, wy = landing(sy, HALF, 1)
        more = wx * wy * DEEP
        block = hr[at + rows : at + SIDE_ROWS[i], :].astype(F32)[:more] * inside
        store_shifts(c3, block, x0, wx, y0, wy)

    for t, (a, b, e) in enumerate(TAP_OFFSETS):
        lanes = slice(t * LANES, (t + 1) * LANES)
        for row, x0, wx, y0, wy in PIECES:
            x1, y1 = x0 + 1 + a, y0 + 1 + b
            rows = wx * wy * DEEP
            window = a3[e + 1, x1 : x1 + wx, y1 : y1 + wy]
            p1[row : row + rows, lanes] = window.reshape(rows, LANES).astype(BF16)
    pre[...] = dot(p1[...], wf[...]) + bias_row[...]

    for parity_x in (0, 1):
        for parity_y in (0, 1):
            total = None
            for a in ((-1, 1) if parity_x else (0,)):
                for b in ((-1, 1) if parity_y else (0,)):
                    x0 = 0 if a == 1 else 1
                    y0 = 0 if b == 1 else 1
                    windows = [
                        c3[1 - e, x0 : x0 + 5, y0 : y0 + 5].reshape(200, LANES).astype(BF16)
                        for e in (-1, 0, 1)
                    ]
                    t = 9 * (a + 1) + 3 * (b + 1)
                    term = dot_nt(
                        jnp.concatenate(windows, 1), db[:, t * LANES : (t + 3) * LANES]
                    )
                    total = term if total is None else total + term
            gs10[:, 1 - parity_x, :, 1 - parity_y] = total.reshape(5, 5, DEEP, LANES)

    pick_live = (iota((LANES, LANES), 0) == C).astype(BF16)
    ten = gs10.reshape(10, 10, DEEP, LANES)
    for row, x0, wx, y0, wy in PIECES:
        rows = wx * wy * DEEP
        value = pre[row : row + rows, :]
        feature = p1[row : row + rows, 13 * LANES : 14 * LANES]
        alive = dot(feature, pick_live)
        gate = 1.0 / (1.0 + jnp.exp(-value))
        summed = (feature.astype(F32) + alive * (value * gate)).astype(BF16).astype(F32)
        grad_sum = ten[x0 : x0 + wx, y0 : y0 + wy].reshape(rows, LANES)
        grad_pre = grad_sum * alive * gate * (1.0 + value * (1.0 - gate))
        store_shifts(s3, summed, x0, wx, y0, wy)
        store_shifts(g3, grad_pre.astype(BF16).astype(F32), x0, wx, y0, wy)

    six = s3.reshape(3, 5, 2, 5, 2, DEEP, LANES)
    for t, (a, b, e) in enumerate(TAP_OFFSETS):
        i0, si = (a + 1) // 2, (a + 1) % 2
        j0, sj = (b + 1) // 2, (b + 1) % 2
        window = six[e + 1, i0 : i0 + 4, si, j0 : j0 + 4, sj]
        ps[:, t * LANES : (t + 1) * LANES] = window.reshape(128, LANES).astype(BF16)
    far_first = (4, 3, 5, 2, 6, 1, 7)
    near_first = (1, 7, 2, 6, 3, 5, 4)

    def rows(which, place):
        start, size = PARTS[which]
        return pl.ds(pl.multiple_of(start + place * 4 * size, 64), 4 * size)

    def block_rows(which, place, x):
        start, size = PARTS[which]
        return pl.ds(pl.multiple_of(start + place * 4 * size + x * size, 16), size)

    order = [(which, j) for j in far_first + (0,) for which in (0, 1)]
    core_copies = []
    for which, j in order:
        there = rows(which, (i_far + j) % 8)
        core_copies.append(
            remote(part.at[1 - core, there], rc.at[there], c_send.at[0], c_recv.at[j], sibling)
        )

    def down_sums():
        cot_turned = c3[1, 1:5, 1:5].reshape(128, LANES).T[0:C].astype(BF16)
        acc = dot(cot_turned, ps[...])
        for j, tile in enumerate(dense_tiles(acc, jnp.zeros((C, LANES), F32))):
            part[1, j * C : (j + 1) * C, :] = tile.astype(BF16)

    def conv_sums():
        pre_turned = g3[1, 1:9, 1:9].reshape(512, LANES).T[0:C].astype(BF16)
        acc = dot(pre_turned, p1[0:512, :])
        for j, tile in enumerate(dense_tiles(acc, acc[:, 13 * LANES : 14 * LANES])):
            part[0, j * C : (j + 1) * C, :] = tile.astype(BF16)

    @pl.when(core == 0)
    def _():
        down_sums()
        for copy in core_copies:
            copy.start()
        conv_sums()

    @pl.when(core == 1)
    def _():
        conv_sums()
        for copy in core_copies:
            copy.start()
        down_sums()

    for which, j in order:
        if which == 0:
            await_bytes(rc.at[0:256], c_recv.at[j])
        here = rows(which, (i_near + j) % 8)
        both = (part[core, here].astype(F32) + rc[here].astype(F32)).astype(BF16)
        if which == 0:
            xa[j] = both.reshape(4, 32, LANES)
            for k in (2, 1, 3):
                remote(
                    xa.at[j, (px + k) % NX], xa_in.at[j, k], xa_send.at[0], xa_recv.at[j], x_peer[k]
                ).start()
        else:
            nb[j] = both
            if j:
                remote(nb.at[j], nb_in.at[j], nb_send.at[0], nb_recv.at[0], near[j]).start()

    for j in far_first + (0,):
        await_bytes(xa_in.at[j, 1:4], xa_recv.at[j])
        total = xa[j, px].astype(F32)
        for k in (1, 3, 2):
            total = total + xa_in[j, k].astype(F32)
        na[j] = total.astype(BF16)
        if j:
            remote(na.at[j], na_in.at[j], na_send.at[0], na_recv.at[0], near[j]).start()
    await_bytes(nb_in.at[1:8], nb_recv.at[0])
    total = nb[0].astype(F32)
    for k in near_first:
        total = total + nb_in[k].astype(F32)
    xb[...] = total.reshape(4, 32, LANES).astype(BF16)
    for k in (2, 1, 3):
        remote(xb.at[(px + k) % NX], xb_in.at[k], xb_send.at[0], xb_recv.at[0], x_peer[k]).start()

    await_bytes(na_in.at[1:8], na_recv.at[0])
    total = na[0].astype(F32)
    for k in near_first:
        total = total + na_in[k].astype(F32)
    far_in[i_far, 0:32] = total.astype(BF16)
    await_bytes(xb_in.at[1:4], xb_recv.at[0])
    total = xb[px].astype(F32)
    for k in (1, 3, 2):
        total = total + xb_in[k].astype(F32)
    far_in[i_far, 32:64] = total.astype(BF16)
    for k in far_first:
        block = far_in.at[i_far]
        remote(block, block, far_send.at[0], far_recv.at[0], far[k]).start()

    downward = (iota((64, 128), 1) == 2 * iota((64, 128), 0)).astype(BF16)
    coarse = (dot(ps[...], df[...]) * cl[...]).astype(BF16)
    down_ref[...] = dot(downward, coarse).astype(BF16)[:, 0:C]

    for t, (a, b, e) in enumerate(TAP_OFFSETS):
        window = g3[1 - e, 1 - a : 9 - a, 1 - b : 9 - b]
        p2[:, t * LANES : (t + 1) * LANES] = window.reshape(512, LANES).astype(BF16)
    grad_in = ten[1:9, 1:9].reshape(512, LANES) + dot_nt(p2[...], wb[...])
    alive = dot(p1[0:512, 13 * LANES : 14 * LANES], pick_live)
    gv_ref[...] = (grad_in * alive).astype(BF16)[:, 0:C]

    await_bytes(far_in.at[0:7], far_recv.at[0])
    total = far_in[0].astype(F32)
    for k in range(1, 8):
        total = total + far_in[k].astype(F32)
    total = total.astype(BF16)

    fin_ref[core, block_rows(0, i_near, px)] = total[0:32]
    fin_ref[core, block_rows(1, i_near, px)] = total[32:64]

    block = fin_ref.at[core, block_rows(0, i_near, px)]
    for k in far_first:
        remote(block, block, gna_send.at[0], gna_recv.at[k], near[k]).start()
    block = fin_ref.at[core, block_rows(1, i_near, px)]
    for k in (2, 1, 3):
        remote(block, block, gxb_send.at[0], gxb_recv.at[0], x_peer[k]).start()

    def across(j):
        if j:
            await_bytes(na_in.at[j], gna_recv.at[j])
        block = fin_ref.at[core, block_rows(0, (i_near - j + 8) % 8, px)]
        for k in (2, 1, 3):
            remote(block, block, gxa_send.at[0], gxa_recv.at[j], x_peer[k]).start()

    def hand_over(which, j):
        if which == 0:
            await_bytes(xa_in.at[j, 1:4], gxa_recv.at[j])
        elif j:
            await_bytes(nb_in.at[j], gnb_recv.at[j])
        block = fin_ref.at[core, rows(which, (i_near - j + 8) % 8)]
        remote(block, block, gc_send.at[0], gc_recv.at[0], sibling).start()

    for j in (0, 1, 7):
        across(j)
    await_bytes(xb_in.at[1:4], gxb_recv.at[0])
    block = fin_ref.at[core, rows(1, i_near)]
    for k in far_first:
        remote(block, block, gnb_send.at[0], gnb_recv.at[k], near[k]).start()
    hand_over(1, 0)
    for j in (2, 6):
        across(j)
    hand_over(0, 0)
    for j in (3, 5, 4):
        across(j)
    for which, j in (
        (0, 1), (0, 7), (1, 1), (1, 7), (0, 2), (0, 6), (1, 2), (1, 6), (0, 3), (0, 5), (0, 4),
        (1, 3), (1, 5), (1, 4),
    ):
        hand_over(which, j)
    for ref, sends in (
        (rc, c_send),
        (xa_in.at[:, 1:4], xa_send),
        (nb_in.at[1:8], nb_send),
        (na_in.at[1:8], na_send),
        (xb_in.at[1:4], xb_send),
        (far_in.at[0:7], far_send),
        (na_in.at[1:8], gna_send),
        (xb_in.at[1:4], gxb_send),
        (xa_in.at[:, 1:4], gxa_send),
        (nb_in.at[1:8], gnb_send),
        (rc, gc_send),
        (rc, gc_recv),
    ):
        await_bytes(ref, sends.at[0])


def finish_kernel(
    factor, fin_ref, down_in, gv_in, down_ref, gv_ref, gc_ref, gb_ref, gd_ref,
    gc, gb, gd, sem,
):
    copies = []

    def send_out(src, dst):
        copies.append(pltpu.make_async_copy(src, dst, sem.at[len(copies)]))
        copies[-1].start()

    send_out(down_in, down_ref)
    send_out(gv_in, gv_ref)
    unit = (iota((LANES, LANES), 0) == iota((LANES, LANES), 1)).astype(BF16)
    for w, held, out in ((1, gd, gd_ref), (0, gc, gc_ref)):
        for j in range(21):
            turned = dot_nt(unit, fin_ref[w, j * C : (j + 1) * C, :]) * factor
            count = min(LANES, TAPS * C - j * LANES)
            held[j * LANES : j * LANES + count, :] = turned[0:count]
            if j % 3 == 2:
                block = pl.ds((j - 2) * LANES, 2 * LANES + count)
                send_out(held.at[block], out.at[block])
        if w == 0:
            gb[...] = turned[32:33]
            send_out(gb, gb_ref)
    for copy in copies:
        copy.wait()


def on_device(voxels, occupancy, conv_weight, conv_bias, down_weight, down_cotangent):
    vmem = pl.BlockSpec(memory_space=pltpu.VMEM)
    anywhere = pl.BlockSpec(memory_space=pl.ANY)
    scratch = [
        ((512, C), BF16),
        ((64, DEEP), jnp.int32),
        ((TAPS, C, C), BF16),
        ((1, C), F32),
        ((TAPS, C, C), BF16),
        ((64, C), BF16),
        ((1, LANES), F32),
        ((HALO_ROWS, LANES), BF16),
        ((HALO_ROWS, LANES), BF16),
        ((3, 12, 12, DEEP, LANES), F32),
        ((3, 6, 6, DEEP, LANES), F32),
        ((5, 2, 5, 2, DEEP, LANES), F32),
        ((3, 10, 10, DEEP, LANES), F32),
        ((3, 10, 10, DEEP, LANES), F32),
        ((800, LANES), F32),
        ((800, K_ALL), BF16),
        ((512, K_ALL), BF16),
        ((128, K_ALL), BF16),
        ((K_ALL, LANES), BF16),
        ((LANES, K_ALL), BF16),
        ((K_ALL, LANES), BF16),
        ((LANES, K_ALL), BF16),
        ((128, LANES), F32),
        ((2, ROWS, LANES), BF16),
        ((ROWS, LANES), BF16),
        ((8, 4, 32, LANES), BF16),
        ((8, 4, 32, LANES), BF16),
        ((8, 128, LANES), BF16),
        ((8, 128, LANES), BF16),
        ((8, 32, LANES), BF16),
        ((8, 32, LANES), BF16),
        ((4, 32, LANES), BF16),
        ((4, 32, LANES), BF16),
        ((8, 64, LANES), BF16),
    ]
    semaphores = [6, 1, 1, 1, 8, 1, 8, 1, 1, 1, 1, 1, 1, 1, 1, 1, 8, 1, 1, 1, 8, 1, 8, 1, 1]
    fin, down, grad_voxels = pl.pallas_call(
        main_kernel,
        out_shape=(
            pltpu.VMEM((2, ROWS, LANES), BF16),
            pltpu.VMEM((64, C), BF16),
            pltpu.VMEM((512, C), BF16),
        ),
        in_specs=[anywhere] * 6,
        out_specs=(vmem, vmem, vmem),
        scratch_shapes=[pltpu.VMEM(shape, dtype) for shape, dtype in scratch]
        + [pltpu.SemaphoreType.DMA((n,)) for n in semaphores],
        compiler_params=pltpu.CompilerParams(
            collective_id=0, has_side_effects=True, vmem_limit_bytes=56 * 1024 * 1024
        ),
    )(
        voxels.reshape(512, C),
        occupancy.reshape(64, DEEP),
        conv_weight,
        conv_bias.reshape(1, C),
        down_weight,
        down_cotangent.reshape(64, C),
    )
    cells = voxels.shape[0] * lax.axis_size("gx") * voxels.shape[1] * lax.axis_size("gy") * DEEP
    factor = 1.0 / math.sqrt(cells)
    down, grad_voxels, grad_conv, grad_bias, grad_down = pl.pallas_call(
        lambda *refs: finish_kernel(factor, *refs),
        out_shape=(
            jax.ShapeDtypeStruct((64, C), BF16),
            jax.ShapeDtypeStruct((512, C), BF16),
            jax.ShapeDtypeStruct((TAPS * C, C), F32),
            jax.ShapeDtypeStruct((1, C), F32),
            jax.ShapeDtypeStruct((TAPS * C, C), F32),
        ),
        in_specs=[vmem] * 3,
        out_specs=(anywhere,) * 5,
        scratch_shapes=[
            pltpu.VMEM((TAPS * C, C), F32),
            pltpu.VMEM((1, C), F32),
            pltpu.VMEM((TAPS * C, C), F32),
            pltpu.SemaphoreType.DMA((17,)),
        ],
        compiler_params=pltpu.CompilerParams(vmem_limit_bytes=32 * 1024 * 1024),
    )(fin, down, grad_voxels)
    return (
        down.reshape(down_cotangent.shape),
        grad_voxels.reshape(voxels.shape),
        grad_conv.reshape(TAPS, C, C),
        grad_bias.reshape(C),
        grad_down.reshape(TAPS, C, C),
    )


def solution(mesh):
    tile = P("gx", "gy", None, None)
    return jax.shard_map(
        on_device,
        mesh=mesh,
        in_specs=(tile, P("gx", "gy", None), P(), P(), P(), tile),
        out_specs=(tile, tile, P(), P(), P()),
        check_vma=False,
    )
```

```python
import math

import jax
import jax.numpy as jnp
from jax import lax
from jax.experimental import pallas as pl
from jax.experimental.pallas import tpu as pltpu
from jax.sharding import PartitionSpec as P

F32 = jnp.float32
BF16 = jnp.bfloat16
MESH = pl.DeviceIdType.MESH

C = 96
LANES = 128
TAPS = 27
TILE = 8
HALF = 4
DEEP = 8
K_ALL = TAPS * LANES
ROWS = 2048
PARTS = ((0, 32), (1024, 32))
NX, NY, NZ = 4, 8, 8
TAP_OFFSETS = [(a, b, e) for a in (-1, 0, 1) for b in (-1, 0, 1) for e in (-1, 0, 1)]

SIDES = [(-1, 0), (1, 0), (0, -1), (0, 1), (-1, -1), (-1, 1), (1, -1), (1, 1)]
SIDE_ROWS = [160 if 0 in side else 48 for side in SIDES]
SIDE_AT = [sum(SIDE_ROWS[:i]) for i in range(8)]
HALO_ROWS = sum(SIDE_ROWS)

PIECES = [
    (0, 1, 8, 1, 8),
    (512, 0, 1, 0, 10),
    (592, 9, 1, 0, 10),
    (672, 1, 8, 0, 1),
    (736, 1, 8, 9, 1),
]


def edge(step, length, width):
    return {-1: (0, width), 0: (0, length), 1: (length - width, width)}[step]


def landing(step, length, width):
    return {-1: (0, width), 0: (width, length), 1: (width + length, width)}[step]


def dot(left, right):
    return lax.dot_general(left, right, (((1,), (0,)), ((), ())), preferred_element_type=F32)


def dot_nt(left, right):
    return lax.dot_general(left, right, (((1,), (1,)), ((), ())), preferred_element_type=F32)


def iota(shape, dim):
    return lax.broadcasted_iota(jnp.int32, shape, dim)


def z_shifts(value):
    columns = value.shape[0]
    level = iota((columns, DEEP, LANES), 1)
    below = jnp.where(level == 0, 0.0, pltpu.roll(value, 1, 1))
    above = jnp.where(level == DEEP - 1, 0.0, pltpu.roll(value, DEEP - 1, 1))
    return below, value, above


def store_shifts(ref, value, at_x, size_x, at_y, size_y):
    for k, shifted in enumerate(z_shifts(value.reshape(size_x * size_y, DEEP, LANES))):
        ref[k, at_x : at_x + size_x, at_y : at_y + size_y] = shifted.reshape(
            size_x, size_y, DEEP, LANES
        )


def dense_tiles(acc, extra):
    lane = iota((C, LANES), 1)
    tap = lambda t: acc[:, t * LANES : (t + 1) * LANES]
    tiles = []
    for group in range(7):
        first = 4 * group
        one = pltpu.roll(tap(first + 1), 96, 1)
        two = pltpu.roll(tap(first + 2), 64, 1)
        tiles.append(jnp.where(lane < 96, tap(first), one))
        tiles.append(jnp.where(lane < 64, one, two))
        if group < 6:
            three = pltpu.roll(tap(first + 3), 32, 1)
        else:
            three = jnp.where(lane == 32, pltpu.roll(extra, 64, 1), 0.0)
        tiles.append(jnp.where(lane < 32, two, three))
    return tiles


def main_kernel(
    vox_hbm, occ_hbm, cw_hbm, bias_hbm, dw_hbm, cot_hbm,
    fin_ref, down_ref, gv_ref,
    vox_ref, occ_ref, cw_ref, bias_ref, dw_ref, cot_ref, bias_row,
    hs, hr, a3, c3, gs10, s3, g3, pre, p1, p2, ps, wf, wb, df, db, cl,
    part, rc, xa, xa_in, nb, nb_in, na, na_in, xb, xb_in, far_in,
    in_sem, h_send, h_recv, c_send, c_recv, xa_send, xa_recv, nb_send, nb_recv,
    na_send, na_recv, xb_send, xb_recv, far_send, far_recv,
    gna_send, gna_recv, gxb_send, gxb_recv, gnb_send, gnb_recv, gxa_send, gxa_recv,
    gc_send, gc_recv,
):
    gx = lax.axis_index("gx")
    gy = lax.axis_index("gy")
    n_gx = lax.axis_size("gx")
    n_gy = lax.axis_size("gy")
    px, pz = gx // NZ, gx % NZ
    py, core = gy // 2, gy % 2
    sibling = (gx, gy + 1 - 2 * core)
    side_peer = [((gx + sx + n_gx) % n_gx, (gy + sy + n_gy) % n_gy) for sx, sy in SIDES]
    x_peer = [(((px + k) % NX) * NZ + pz, gy) for k in range(NX)]
    y_peer = [(gx, ((py + k) % NY) * 2 + core) for k in range(NY)]
    z_peer = [(px * NZ + (pz + k) % NZ, gy) for k in range(NZ)]

    def chosen(first, second):
        return tuple(i + core * (j - i) for i, j in zip(first, second))

    near = [chosen(y_peer[k], z_peer[k]) for k in range(8)]
    far = [chosen(z_peer[k], y_peer[k]) for k in range(8)]
    i_near = py + core * (pz - py)
    i_far = pz + core * (py - pz)

    barrier = pltpu.get_barrier_semaphore()
    greeted = [peer for k in (4, 3, 5, 2, 6) for peer in (y_peer[k], z_peer[k])]
    greeted += [x_peer[2]] + side_peer[4:] + [x_peer[1], x_peer[3]]
    greeted += [y_peer[1], z_peer[1], y_peer[7], z_peer[7]] + side_peer[:4]
    for peer in greeted:
        pl.semaphore_signal(barrier, inc=1, device_id=peer, device_id_type=MESH)

    loads = [
        pltpu.make_async_copy(src, dst, in_sem.at[i])
        for i, (src, dst) in enumerate(
            (
                (occ_hbm, occ_ref),
                (vox_hbm, vox_ref),
                (cot_hbm, cot_ref),
                (cw_hbm, cw_ref),
                (dw_hbm, dw_ref),
                (bias_hbm, bias_ref),
            )
        )
    ]
    for load in loads:
        load.start()

    def remote(src, dst, send, recv, peer):
        return pltpu.make_async_remote_copy(
            src_ref=src, dst_ref=dst, send_sem=send, recv_sem=recv, device_id=peer,
            device_id_type=MESH,
        )

    def await_bytes(ref, semaphore):
        pltpu.make_async_copy(ref, ref, semaphore).wait()

    for load in loads[:3]:
        load.wait()

    spread = (iota((512, 64), 0) // DEEP == iota((512, 64), 1)).astype(BF16)
    by_column = dot(spread, occ_ref[...].astype(F32).astype(BF16))
    own_level = iota((512, DEEP), 0) % DEEP == iota((512, DEEP), 1)
    picked = jnp.where(own_level, by_column, 0.0).astype(BF16)
    live = dot(picked, jnp.ones((DEEP, LANES), BF16))
    widen = (iota((C, LANES), 0) == iota((C, LANES), 1)).astype(BF16)
    lane512 = iota((512, LANES), 1)
    masked = jnp.where(lane512 == C, live, dot(vox_ref[...], widen) * live)
    masked = masked.reshape(TILE, TILE, DEEP, LANES)
    pairs = live.reshape(HALF, 2, HALF, 2, DEEP, LANES)
    most = jnp.maximum(
        jnp.maximum(pairs[:, 0, :, 0], pairs[:, 0, :, 1]),
        jnp.maximum(pairs[:, 1, :, 0], pairs[:, 1, :, 1]),
    ).reshape(HALF * HALF, DEEP, LANES)
    coarse_live = jnp.maximum(most, pltpu.roll(most, DEEP - 1, 1)).reshape(128, LANES)
    cl[...] = coarse_live
    upward = (iota((128, 64), 0) == 2 * iota((128, 64), 1)).astype(BF16)
    cot = (dot(upward, dot(cot_ref[...], widen).astype(BF16)) * coarse_live).reshape(
        HALF, HALF, DEEP, LANES
    )

    for i, (sx, sy) in enumerate(SIDES):
        x0, wx = edge(sx, TILE, 2)
        y0, wy = edge(sy, TILE, 2)
        rows = wx * wy * DEEP
        at = SIDE_AT[i]
        hs[at : at + rows, :] = (
            masked[x0 : x0 + wx, y0 : y0 + wy].reshape(rows, LANES).astype(BF16)
        )
        x0, wx = edge(sx, HALF, 1)
        y0, wy = edge(sy, HALF, 1)
        more = wx * wy * DEEP
        block = cot[x0 : x0 + wx, y0 : y0 + wy].reshape(more, LANES)
        if more < 16:
            block = jnp.concatenate([block, jnp.zeros((16 - more, LANES), F32)], 0)
        hs[at + rows : at + SIDE_ROWS[i], :] = block.astype(BF16)

    pl.semaphore_wait(barrier, len(greeted))
    for i in (4, 5, 6, 7, 0, 1, 2, 3):
        sx, sy = SIDES[i]
        there = SIDES.index((-sx, -sy))
        mine = pl.ds(SIDE_AT[i], SIDE_ROWS[i])
        theirs = pl.ds(SIDE_AT[there], SIDE_ROWS[i])
        copy = remote(hs.at[mine], hr.at[theirs], h_send.at[0], h_recv.at[0], side_peer[i])
        copy.start()

    store_shifts(a3, masked, 2, TILE, 2, TILE)
    store_shifts(c3, cot, 1, HALF, 1, HALF)
    for ref in (wf, wb, df, db):
        ref[...] = jnp.zeros(ref.shape, BF16)
    bias_row[...] = jnp.zeros((1, LANES), F32)
    for load in loads[3:]:
        load.wait()
    bias_row[:, 0:C] = bias_ref[...]
    for t in range(TAPS):
        for source, plain, turned in ((cw_ref, wf, wb), (dw_ref, df, db)):
            block = source[t]
            plain[t * LANES : t * LANES + C, 0:C] = block
            turned[0:C, t * LANES : t * LANES + C] = block
    for w in (0, 1):
        part[w, 2016:2048, :] = jnp.zeros((32, LANES), BF16)

    await_bytes(hs, h_send.at[0])
    await_bytes(hr, h_recv.at[0])
    for i, (sx, sy) in enumerate(SIDES):
        inside = 1.0
        for step, at, size in ((sx, gx, n_gx), (sy, gy, n_gy)):
            if step:
                inside = inside * jnp.where(at == (0 if step < 0 else size - 1), 0.0, 1.0)
        at = SIDE_AT[i]
        x0, wx = landing(sx, TILE, 2)
        y0, wy = landing(sy, TILE, 2)
        rows = wx * wy * DEEP
        store_shifts(a3, hr[at : at + rows, :].astype(F32) * inside, x0, wx, y0, wy)
        x0, wx = landing(sx, HALF, 1)
        y0, wy = landing(sy, HALF, 1)
        more = wx * wy * DEEP
        block = hr[at + rows : at + SIDE_ROWS[i], :].astype(F32)[:more] * inside
        store_shifts(c3, block, x0, wx, y0, wy)

    for t, (a, b, e) in enumerate(TAP_OFFSETS):
        lanes = slice(t * LANES, (t + 1) * LANES)
        for row, x0, wx, y0, wy in PIECES:
            x1, y1 = x0 + 1 + a, y0 + 1 + b
            rows = wx * wy * DEEP
            window = a3[e + 1, x1 : x1 + wx, y1 : y1 + wy]
            p1[row : row + rows, lanes] = window.reshape(rows, LANES).astype(BF16)
    pre[...] = dot(p1[...], wf[...]) + bias_row[...]

    for parity_x in (0, 1):
        for parity_y in (0, 1):
            total = None
            for a in ((-1, 1) if parity_x else (0,)):
                for b in ((-1, 1) if parity_y else (0,)):
                    x0 = 0 if a == 1 else 1
                    y0 = 0 if b == 1 else 1
                    windows = [
                        c3[1 - e, x0 : x0 + 5, y0 : y0 + 5].reshape(200, LANES).astype(BF16)
                        for e in (-1, 0, 1)
                    ]
                    t = 9 * (a + 1) + 3 * (b + 1)
                    term = dot_nt(
                        jnp.concatenate(windows, 1), db[:, t * LANES : (t + 3) * LANES]
                    )
                    total = term if total is None else total + term
            gs10[:, 1 - parity_x, :, 1 - parity_y] = total.reshape(5, 5, DEEP, LANES)

    pick_live = (iota((LANES, LANES), 0) == C).astype(BF16)
    ten = gs10.reshape(10, 10, DEEP, LANES)
    for row, x0, wx, y0, wy in PIECES:
        rows = wx * wy * DEEP
        value = pre[row : row + rows, :]
        feature = p1[row : row + rows, 13 * LANES : 14 * LANES]
        alive = dot(feature, pick_live)
        gate = 1.0 / (1.0 + jnp.exp(-value))
        summed = (feature.astype(F32) + alive * (value * gate)).astype(BF16).astype(F32)
        grad_sum = ten[x0 : x0 + wx, y0 : y0 + wy].reshape(rows, LANES)
        grad_pre = grad_sum * alive * gate * (1.0 + value * (1.0 - gate))
        store_shifts(s3, summed, x0, wx, y0, wy)
        store_shifts(g3, grad_pre.astype(BF16).astype(F32), x0, wx, y0, wy)

    six = s3.reshape(3, 5, 2, 5, 2, DEEP, LANES)
    for t, (a, b, e) in enumerate(TAP_OFFSETS):
        i0, si = (a + 1) // 2, (a + 1) % 2
        j0, sj = (b + 1) // 2, (b + 1) % 2
        window = six[e + 1, i0 : i0 + 4, si, j0 : j0 + 4, sj]
        ps[:, t * LANES : (t + 1) * LANES] = window.reshape(128, LANES).astype(BF16)
    far_first = (4, 3, 5, 2, 6, 1, 7)
    near_first = (1, 7, 2, 6, 3, 5, 4)

    def rows(which, place):
        start, size = PARTS[which]
        return pl.ds(pl.multiple_of(start + place * 4 * size, 64), 4 * size)

    def block_rows(which, place, x):
        start, size = PARTS[which]
        return pl.ds(pl.multiple_of(start + place * 4 * size + x * size, 16), size)

    order = [(which, j) for j in far_first + (0,) for which in (1, 0)]
    core_copies = []
    for which, j in order:
        there = rows(which, (i_far + j) % 8)
        core_copies.append(
            remote(part.at[1 - core, there], rc.at[there], c_send.at[0], c_recv.at[j], sibling)
        )

    def down_sums():
        cot_turned = c3[1, 1:5, 1:5].reshape(128, LANES).T[0:C].astype(BF16)
        acc = dot(cot_turned, ps[...])
        for j, tile in enumerate(dense_tiles(acc, jnp.zeros((C, LANES), F32))):
            part[1, j * C : (j + 1) * C, :] = tile.astype(BF16)

    def conv_sums():
        pre_turned = g3[1, 1:9, 1:9].reshape(512, LANES).T[0:C].astype(BF16)
        acc = dot(pre_turned, p1[0:512, :])
        for j, tile in enumerate(dense_tiles(acc, acc[:, 13 * LANES : 14 * LANES])):
            part[0, j * C : (j + 1) * C, :] = tile.astype(BF16)

    @pl.when(core == 0)
    def _():
        down_sums()
        for copy in core_copies:
            copy.start()
        conv_sums()

    @pl.when(core == 1)
    def _():
        conv_sums()
        for copy in core_copies:
            copy.start()
        down_sums()

    for which, j in order:
        if which == 1:
            await_bytes(rc.at[0:256], c_recv.at[j])
        here = rows(which, (i_near + j) % 8)
        both = (part[core, here].astype(F32) + rc[here].astype(F32)).astype(BF16)
        if which == 0:
            xa[j] = both.reshape(4, 32, LANES)
            for k in (2, 1, 3):
                remote(
                    xa.at[j, (px + k) % NX], xa_in.at[j, k], xa_send.at[0], xa_recv.at[j], x_peer[k]
                ).start()
        else:
            nb[j] = both
            if j:
                remote(nb.at[j], nb_in.at[j], nb_send.at[0], nb_recv.at[0], near[j]).start()

    for j in far_first + (0,):
        await_bytes(xa_in.at[j, 1:4], xa_recv.at[j])
        total = xa[j, px].astype(F32)
        for k in (1, 3, 2):
            total = total + xa_in[j, k].astype(F32)
        na[j] = total.astype(BF16)
        if j:
            remote(na.at[j], na_in.at[j], na_send.at[0], na_recv.at[0], near[j]).start()
    await_bytes(nb_in.at[1:8], nb_recv.at[0])
    total = nb[0].astype(F32)
    for k in near_first:
        total = total + nb_in[k].astype(F32)
    xb[...] = total.reshape(4, 32, LANES).astype(BF16)
    for k in (2, 1, 3):
        remote(xb.at[(px + k) % NX], xb_in.at[k], xb_send.at[0], xb_recv.at[0], x_peer[k]).start()

    await_bytes(na_in.at[1:8], na_recv.at[0])
    total = na[0].astype(F32)
    for k in near_first:
        total = total + na_in[k].astype(F32)
    far_in[i_far, 0:32] = total.astype(BF16)
    await_bytes(xb_in.at[1:4], xb_recv.at[0])
    total = xb[px].astype(F32)
    for k in (1, 3, 2):
        total = total + xb_in[k].astype(F32)
    far_in[i_far, 32:64] = total.astype(BF16)
    for k in far_first:
        block = far_in.at[i_far]
        remote(block, block, far_send.at[0], far_recv.at[0], far[k]).start()

    downward = (iota((64, 128), 1) == 2 * iota((64, 128), 0)).astype(BF16)
    coarse = (dot(ps[...], df[...]) * cl[...]).astype(BF16)
    down_ref[...] = dot(downward, coarse).astype(BF16)[:, 0:C]

    for t, (a, b, e) in enumerate(TAP_OFFSETS):
        window = g3[1 - e, 1 - a : 9 - a, 1 - b : 9 - b]
        p2[:, t * LANES : (t + 1) * LANES] = window.reshape(512, LANES).astype(BF16)
    grad_in = ten[1:9, 1:9].reshape(512, LANES) + dot_nt(p2[...], wb[...])
    alive = dot(p1[0:512, 13 * LANES : 14 * LANES], pick_live)
    gv_ref[...] = (grad_in * alive).astype(BF16)[:, 0:C]

    await_bytes(far_in.at[0:7], far_recv.at[0])
    total = far_in[0].astype(F32)
    for k in range(1, 8):
        total = total + far_in[k].astype(F32)
    total = total.astype(BF16)

    fin_ref[core, block_rows(0, i_near, px)] = total[0:32]
    fin_ref[core, block_rows(1, i_near, px)] = total[32:64]

    block = fin_ref.at[core, block_rows(1, i_near, px)]
    for k in (2, 1, 3):
        remote(block, block, gxb_send.at[0], gxb_recv.at[0], x_peer[k]).start()
    block = fin_ref.at[core, block_rows(0, i_near, px)]
    for k in far_first:
        remote(block, block, gna_send.at[0], gna_recv.at[k], near[k]).start()

    def across(j):
        if j:
            await_bytes(na_in.at[j], gna_recv.at[j])
        block = fin_ref.at[core, block_rows(0, (i_near - j + 8) % 8, px)]
        for k in (2, 1, 3):
            remote(block, block, gxa_send.at[0], gxa_recv.at[j], x_peer[k]).start()

    def hand_over(which, j):
        if which == 0:
            await_bytes(xa_in.at[j, 1:4], gxa_recv.at[j])
        elif j:
            await_bytes(nb_in.at[j], gnb_recv.at[j])
        block = fin_ref.at[core, rows(which, (i_near - j + 8) % 8)]
        remote(block, block, gc_send.at[0], gc_recv.at[0], sibling).start()

    for j in (0, 1, 7):
        across(j)
    await_bytes(xb_in.at[1:4], gxb_recv.at[0])
    block = fin_ref.at[core, rows(1, i_near)]
    for k in far_first:
        remote(block, block, gnb_send.at[0], gnb_recv.at[k], near[k]).start()
    hand_over(1, 0)
    for j in (2, 6):
        across(j)
    hand_over(0, 0)
    for j in (3, 5, 4):
        across(j)
    for which, j in (
        (0, 1), (0, 7), (1, 1), (1, 7), (0, 2), (0, 6), (1, 2), (1, 6), (0, 3), (0, 5), (0, 4),
        (1, 3), (1, 5), (1, 4),
    ):
        hand_over(which, j)
    for ref, sends in (
        (rc, c_send),
        (xa_in.at[:, 1:4], xa_send),
        (nb_in.at[1:8], nb_send),
        (na_in.at[1:8], na_send),
        (xb_in.at[1:4], xb_send),
        (far_in.at[0:7], far_send),
        (na_in.at[1:8], gna_send),
        (xb_in.at[1:4], gxb_send),
        (xa_in.at[:, 1:4], gxa_send),
        (nb_in.at[1:8], gnb_send),
        (rc, gc_send),
        (rc, gc_recv),
    ):
        await_bytes(ref, sends.at[0])


def finish_kernel(
    factor, fin_ref, down_in, gv_in, down_ref, gv_ref, gc_ref, gb_ref, gd_ref,
    gc, gb, gd, sem,
):
    copies = []

    def send_out(src, dst):
        copies.append(pltpu.make_async_copy(src, dst, sem.at[len(copies)]))
        copies[-1].start()

    send_out(down_in, down_ref)
    send_out(gv_in, gv_ref)
    unit = (iota((LANES, LANES), 0) == iota((LANES, LANES), 1)).astype(BF16)
    for w, held, out in ((1, gd, gd_ref), (0, gc, gc_ref)):
        for j in range(21):
            turned = dot_nt(unit, fin_ref[w, j * C : (j + 1) * C, :]) * factor
            count = min(LANES, TAPS * C - j * LANES)
            held[j * LANES : j * LANES + count, :] = turned[0:count]
            if j % 3 == 2:
                block = pl.ds((j - 2) * LANES, 2 * LANES + count)
                send_out(held.at[block], out.at[block])
        if w == 0:
            gb[...] = turned[32:33]
            send_out(gb, gb_ref)
    for copy in copies:
        copy.wait()


def on_device(voxels, occupancy, conv_weight, conv_bias, down_weight, down_cotangent):
    vmem = pl.BlockSpec(memory_space=pltpu.VMEM)
    anywhere = pl.BlockSpec(memory_space=pl.ANY)
    scratch = [
        ((512, C), BF16),
        ((64, DEEP), jnp.int32),
        ((TAPS, C, C), BF16),
        ((1, C), F32),
        ((TAPS, C, C), BF16),
        ((64, C), BF16),
        ((1, LANES), F32),
        ((HALO_ROWS, LANES), BF16),
        ((HALO_ROWS, LANES), BF16),
        ((3, 12, 12, DEEP, LANES), F32),
        ((3, 6, 6, DEEP, LANES), F32),
        ((5, 2, 5, 2, DEEP, LANES), F32),
        ((3, 10, 10, DEEP, LANES), F32),
        ((3, 10, 10, DEEP, LANES), F32),
        ((800, LANES), F32),
        ((800, K_ALL), BF16),
        ((512, K_ALL), BF16),
        ((128, K_ALL), BF16),
        ((K_ALL, LANES), BF16),
        ((LANES, K_ALL), BF16),
        ((K_ALL, LANES), BF16),
        ((LANES, K_ALL), BF16),
        ((128, LANES), F32),
        ((2, ROWS, LANES), BF16),
        ((ROWS, LANES), BF16),
        ((8, 4, 32, LANES), BF16),
        ((8, 4, 32, LANES), BF16),
        ((8, 128, LANES), BF16),
        ((8, 128, LANES), BF16),
        ((8, 32, LANES), BF16),
        ((8, 32, LANES), BF16),
        ((4, 32, LANES), BF16),
        ((4, 32, LANES), BF16),
        ((8, 64, LANES), BF16),
    ]
    semaphores = [6, 1, 1, 1, 8, 1, 8, 1, 1, 1, 1, 1, 1, 1, 1, 1, 8, 1, 1, 1, 8, 1, 8, 1, 1]
    fin, down, grad_voxels = pl.pallas_call(
        main_kernel,
        out_shape=(
            pltpu.VMEM((2, ROWS, LANES), BF16),
            pltpu.VMEM((64, C), BF16),
            pltpu.VMEM((512, C), BF16),
        ),
        in_specs=[anywhere] * 6,
        out_specs=(vmem, vmem, vmem),
        scratch_shapes=[pltpu.VMEM(shape, dtype) for shape, dtype in scratch]
        + [pltpu.SemaphoreType.DMA((n,)) for n in semaphores],
        compiler_params=pltpu.CompilerParams(
            collective_id=0, has_side_effects=True, vmem_limit_bytes=56 * 1024 * 1024
        ),
    )(
        voxels.reshape(512, C),
        occupancy.reshape(64, DEEP),
        conv_weight,
        conv_bias.reshape(1, C),
        down_weight,
        down_cotangent.reshape(64, C),
    )
    cells = voxels.shape[0] * lax.axis_size("gx") * voxels.shape[1] * lax.axis_size("gy") * DEEP
    factor = 1.0 / math.sqrt(cells)
    down, grad_voxels, grad_conv, grad_bias, grad_down = pl.pallas_call(
        lambda *refs: finish_kernel(factor, *refs),
        out_shape=(
            jax.ShapeDtypeStruct((64, C), BF16),
            jax.ShapeDtypeStruct((512, C), BF16),
            jax.ShapeDtypeStruct((TAPS * C, C), F32),
            jax.ShapeDtypeStruct((1, C), F32),
            jax.ShapeDtypeStruct((TAPS * C, C), F32),
        ),
        in_specs=[vmem] * 3,
        out_specs=(anywhere,) * 5,
        scratch_shapes=[
            pltpu.VMEM((TAPS * C, C), F32),
            pltpu.VMEM((1, C), F32),
            pltpu.VMEM((TAPS * C, C), F32),
            pltpu.SemaphoreType.DMA((17,)),
        ],
        compiler_params=pltpu.CompilerParams(vmem_limit_bytes=32 * 1024 * 1024),
    )(fin, down, grad_voxels)
    return (
        down.reshape(down_cotangent.shape),
        grad_voxels.reshape(voxels.shape),
        grad_conv.reshape(TAPS, C, C),
        grad_bias.reshape(C),
        grad_down.reshape(TAPS, C, C),
    )


def solution(mesh):
    tile = P("gx", "gy", None, None)
    return jax.shard_map(
        on_device,
        mesh=mesh,
        in_specs=(tile, P("gx", "gy", None), P(), P(), P(), tile),
        out_specs=(tile, tile, P(), P(), P()),
        check_vma=False,
    )
```
